256 devices in a mesh: dp: 16 (over x_hi, y, core), tensor: 16 (over x_lo, z).
Axes of the slice: x: 4 (x_hi: 2, x_lo: 2; x = x_hi * 2 + x_lo), y: 4, z: 8, core: 2. Of those that a mesh axis runs over, the one named last changes fastest.
Arguments:
- tokens_in: bfloat16 [2048, 8192], P('dp'), may hold values from -6 to 6
- proj_gate: bfloat16 [8192, 8192], P('dp', 'tensor'), may hold values from -0.0625 to 0.0625
- proj_value: bfloat16 [8192, 8192], P('dp', 'tensor')
- state_in: bfloat16 [8192, 128], P('tensor'), may hold values from -0.0625 to 0.0625
- state_out: bfloat16 [8192, 128], P('tensor'), may hold values from -0.0625 to 0.0625
- proj_step: bfloat16 [8192, 128], P('tensor'), may hold values from -0.0625 to 0.0625
- step_bias: float32 [128], P('tensor'), may hold values from -4 to -1
- decay_log: float32 [128], P('tensor'), may hold values from -1 to 1.5
- skip_scale: float32 [128], P('tensor'), may hold values from 0.5 to 1.5
- norm_gain: float32 [8192], P('tensor'), may hold values from 0.5 to 1.5
- proj_output: bfloat16 [8192, 8192], P('dp', 'tensor'), may hold values from -0.0625 to 0.0625
- upstream: bfloat16 [2048, 8192], P('dp'), may hold values from -6 to 6
Outputs:
- layer_out: bfloat16 [2048, 8192], P('dp')
- input_grad: bfloat16 [2048, 8192], P('dp')
- grad_gate: float32 [8192, 8192], P('dp', 'tensor')
- grad_value: float32 [8192, 8192], P('dp', 'tensor')
- grad_output: float32 [8192, 8192], P('dp', 'tensor')
- grad_state_in: float32 [8192, 128], P('tensor')
- grad_state_out: float32 [8192, 128], P('tensor')
- grad_step: float32 [8192, 128], P('tensor')
- grad_bias: float32 [128], P('tensor')
- grad_decay: float32 [128], P('tensor')
- grad_skip: float32 [128], P('tensor')
- grad_gain: float32 [8192], P('tensor')
The draws below stay inside these ranges and needn't reach their ends.
All inputs are finite; a program needn't handle non-finite values.
Results may differ from the reference program's by a relative error of at most 0.0051.
Values may be sent and summed in bfloat16 or wider, within the bound.
A program may use at most 192 MiB of HBM per device.

```python
import jax
import jax.numpy as jnp
from jax import lax

D = 8192
HEADS = 128
HDIM = 64
STATE = 128
TOK_DEV = 128
TOKENS = 2048
INNER = 8192
N_DP = 16


def draw_proj_value(key, part):
    key = jax.random.fold_in(key, 7)
    columns = HEADS * HDIM
    base = jax.random.normal(key, (D, columns), jnp.float32) * D ** (-0.5)
    ramp = jnp.arange(columns, dtype=jnp.float32) / columns
    result = base * (3.0 ** ramp)[None, :]
    return result.astype(jnp.bfloat16)


def strengthened(values, rng, source, target, blocks, factor):
    def block_of(axis_at):
        return (jnp.arange(values.shape[axis_at]) // (values.shape[axis_at] // blocks)).reshape((-1,) + (1,) * (values.ndim - 1 - axis_at))

    near = jax.random.permutation(rng, blocks)[block_of(target)]
    far = (block_of(target) + blocks // 2) % blocks
    return jnp.where((block_of(source) == near) | (block_of(source) == far), factor * values, values)


def levels(own_key, shape, pieces, low, largest):
    factor_of = 1.0
    for dim, parts in pieces:
        draws = jax.random.uniform(jax.random.fold_in(jax.random.fold_in(own_key, 6), dim), (parts,), jnp.float32, low / len(pieces), largest / len(pieces))
        factor_of = factor_of * jnp.repeat(jnp.exp(draws), shape[dim] // parts).reshape((-1,) + (1,) * (len(shape) - 1 - dim))
    return factor_of


def bell_draw(key, dims, deviation, most, cuts=(), kind=jnp.bfloat16):
    values = deviation * jax.random.normal(key, dims, jnp.float32)
    if cuts:
        values = values * levels(key, dims, cuts, -0.22, 0.18)
    return jnp.clip(values, -most, most).astype(kind)


def bell_draw_with(stream_key, extent, width, limit, pieces, heavy, held_as=jnp.bfloat16):
    values = width * jax.random.normal(stream_key, extent, jnp.float32)
    if pieces:
        values = values * levels(stream_key, extent, pieces, -0.22, 0.18)
    return jnp.clip(strengthened(values, jax.random.fold_in(stream_key, 3), *heavy), -limit, limit).astype(held_as)


def setup_inputs(seed: int = 0) -> dict:
    splits = jax.random.split(jax.random.key(seed), 13)
    tokens_in = bell_draw_with(splits[0], (TOKENS, D), 1.0, 6.0, ((0, 16),), (0, 1, 16, 2.0))
    proj_gate = bell_draw(splits[1], (D, INNER), D ** -0.5, 0.0625, ((0, 16), (1, 16)))
    proj_value = draw_proj_value(jax.random.fold_in(splits[12], 71), 0)
    state_in = bell_draw(splits[3], (D, STATE), D ** -0.5, 0.0625, ((0, 16),))
    state_out = bell_draw(splits[4], (D, STATE), D ** -0.5, 0.0625, ((0, 16),))
    proj_step = bell_draw(splits[5], (D, HEADS), D ** -0.5, 0.0625, ((0, 16),))
    step_bias = jnp.clip(-4.0 + 3.0 * jax.random.uniform(splits[6], (HEADS,), jnp.float32) ** levels(splits[6], (HEADS,), ((0, 16),), -0.2, 0.2), -4.0, -1.0)
    decay_log = jnp.clip(-1.0 + 2.5 * jax.random.uniform(splits[7], (HEADS,), jnp.float32) ** levels(splits[7], (HEADS,), ((0, 16),), -0.2, 0.2), -1.0, 1.5)
    skip_scale = jnp.clip(0.5 + 1.0 * jax.random.uniform(splits[8], (HEADS,), jnp.float32) ** levels(splits[8], (HEADS,), ((0, 16),), -0.2, 0.2), 0.5, 1.5)
    norm_gain = jnp.clip(0.5 + 1.0 * jax.random.uniform(splits[9], (INNER,), jnp.float32) ** levels(splits[9], (INNER,), ((0, 16),), -0.2, 0.2), 0.5, 1.5)
    proj_output = bell_draw(splits[10], (D, INNER), INNER ** -0.5, 0.0625, ((0, 16), (1, 16)))
    upstream = bell_draw_with(splits[11], (TOKENS, D), 1.0, 6.0, ((0, 16),), (0, 1, 16, 2.0))
    return {"tokens_in": tokens_in, "proj_gate": proj_gate, "proj_value": proj_value, "state_in": state_in, "state_out": state_out, "proj_step": proj_step, "step_bias": step_bias, "decay_log": decay_log, "skip_scale": skip_scale, "norm_gain": norm_gain, "proj_output": proj_output, "upstream": upstream}


HIGH = lax.Precision.HIGHEST
EPS = 1e-05

def state_mix(gate_pre, value_pre, mat_b, mat_c, step_raw, step_bias, decay_log, skip_scale):
    length = value_pre.shape[0]
    heads = step_raw.shape[1]
    step_size = jax.nn.softplus(step_raw + step_bias)
    rate = jnp.exp(decay_log) * step_size
    cumulative = jnp.cumsum(rate, axis=0)
    affinity = jnp.dot(mat_c, mat_b.T, precision=HIGH)
    position = jnp.arange(length)
    causal = (position[:, None] >= position[None, :])[:, :, None]
    spread = cumulative[:, None, :] - cumulative[None, :, :]
    spread = jnp.where(causal, spread, jnp.float32(0.0))
    kernel = jnp.where(causal, jnp.exp(-spread), jnp.float32(0.0)) * affinity[:, :, None] * step_size[None, :, :]
    per_head = value_pre.reshape(length, heads, -1)
    outputs = jnp.einsum('tsh,shp->thp', kernel, per_head, precision=HIGH) + skip_scale[None, :, None] * per_head
    return outputs.reshape(length, -1) * jax.nn.silu(gate_pre)

def all_sequences(gate_pre, value_pre, mat_b, mat_c, step_raw, step_bias, decay_log, skip_scale):

    def split(array):
        return array.reshape((N_DP, TOK_DEV) + array.shape[1:])
    mapped = jax.vmap(state_mix, in_axes=(0, 0, 0, 0, 0, None, None, None))
    result = mapped(split(gate_pre), split(value_pre), split(mat_b), split(mat_c), split(step_raw), step_bias, decay_log, skip_scale)
    return result.reshape(TOKENS, -1)

def reference(tokens_in, proj_gate, proj_value, state_in, state_out, proj_step, step_bias, decay_log, skip_scale, norm_gain, proj_output, upstream):
    inner = HEADS * HDIM
    f32 = jnp.float32
    bf16 = jnp.bfloat16
    gate_pre = jnp.dot(tokens_in, proj_gate, preferred_element_type=f32)
    value_pre = jnp.dot(tokens_in, proj_value, preferred_element_type=f32)
    mat_b = jnp.dot(tokens_in, state_in, preferred_element_type=f32)
    mat_c = jnp.dot(tokens_in, state_out, preferred_element_type=f32)
    step_raw = jnp.dot(tokens_in, proj_step, preferred_element_type=f32)
    gated, pull = jax.vjp(all_sequences, gate_pre, value_pre, mat_b, mat_c, step_raw, step_bias, decay_log, skip_scale)
    inv_rms = lax.rsqrt(lax.optimization_barrier(jnp.mean(gated * gated, axis=1)) + EPS)
    normed = (gated * inv_rms[:, None] * norm_gain).astype(bf16)
    layer_out = jnp.dot(normed, proj_output.T, preferred_element_type=f32).astype(bf16)
    grad_normed = jnp.dot(upstream, proj_output, preferred_element_type=f32)
    grad_output = jnp.dot(upstream.T, normed, preferred_element_type=f32)
    grad_gain = lax.optimization_barrier(jnp.sum(grad_normed * gated * inv_rms[:, None], axis=0))
    scaled = grad_normed * norm_gain
    dot_total = lax.optimization_barrier(jnp.sum(scaled * gated, axis=1))
    grad_gated = inv_rms[:, None] * scaled - gated * (inv_rms ** 3 * dot_total / inner)[:, None]
    gate_back, value_back, back_b, back_c, step_back, grad_bias, grad_decay, grad_skip = pull(grad_gated)
    gate_low = gate_back.astype(bf16)
    value_low = value_back.astype(bf16)
    b_low = back_b.astype(bf16)
    c_low = back_c.astype(bf16)
    step_low = step_back.astype(bf16)
    grad_gate = jnp.dot(tokens_in.T, gate_low, preferred_element_type=f32)
    grad_value = jnp.dot(tokens_in.T, value_low, preferred_element_type=f32)
    grad_state_in = jnp.dot(tokens_in.T, b_low, preferred_element_type=f32)
    grad_state_out = jnp.dot(tokens_in.T, c_low, preferred_element_type=f32)
    grad_step = jnp.dot(tokens_in.T, step_low, preferred_element_type=f32)
    side_back = jnp.dot(b_low, state_in.T, preferred_element_type=f32) + jnp.dot(c_low, state_out.T, preferred_element_type=f32) + jnp.dot(step_low, proj_step.T, preferred_element_type=f32)
    dense = jnp.dot(gate_low, proj_gate.T, preferred_element_type=f32) + jnp.dot(value_low, proj_value.T, preferred_element_type=f32)
    input_grad = (dense + side_back).astype(bf16)
    return (layer_out, input_grad, grad_gate, grad_value, grad_output, grad_state_in, grad_state_out, grad_step, grad_bias, grad_decay, grad_skip, grad_gain)
```

```python
import jax
import jax.numpy as jnp
from jax import lax
from jax.experimental import pallas as pl
from jax.experimental.pallas import tpu as pltpu
from jax.sharding import PartitionSpec as P

MESH = pl.DeviceIdType.MESH
HIGH = lax.Precision.HIGHEST
EPS = 1e-05
INNER = 8192
F32 = jnp.float32
BF16 = jnp.bfloat16
VMEM_LIMIT = 58 * 2**20


def coords():
    d = lax.axis_index("dp")
    t = lax.axis_index("tensor")
    return d // 8, (d // 2) % 4, d % 2, t // 8, t % 8


def place(x_hi, y, core, x_lo, z):
    return (x_hi * 8 + y * 2 + core, x_lo * 8 + z)


def announce(devices):
    barrier = pltpu.get_barrier_semaphore()
    for device in devices:
        pl.semaphore_signal(barrier, inc=1, device_id=device, device_id_type=MESH)


def gathered(count):
    pl.semaphore_wait(pltpu.get_barrier_semaphore(), count)


def chip_peer(j):
    x_hi, y, core, x_lo, z = coords()
    return place((x_hi + j // 4) % 2, (y + j % 4) % 4, core, x_lo, z)


def core_peer():
    x_hi, y, core, x_lo, z = coords()
    return place(x_hi, y, 1 - core, x_lo, z)


def tensor_peer(j):
    x_hi, y, core, x_lo, z = coords()
    return place(x_hi, y, core, (x_lo + j // 8) % 2, (z + j % 8) % 8)


def tensor_place(j):
    x_hi, y, core, x_lo, z = coords()
    return ((x_lo + j // 8) % 2) * 8 + (z + j % 8) % 8


def drive(steps, count=1):
    for _ in range(count):
        next(steps, None)


def finish(steps):
    for _ in steps:
        pass


def remote(src, dst, send, recv, device):
    return pltpu.make_async_remote_copy(
        src_ref=src, dst_ref=dst, send_sem=send, recv_sem=recv, device_id=device, device_id_type=MESH
    )


def dot(a, b):
    return jnp.dot(a, b, preferred_element_type=F32)


def dot_rows(a, b):
    return lax.dot_general(a, b, (((0,), (0,)), ((), ())), preferred_element_type=F32)


def dot_cols(a, b):
    return lax.dot_general(a, b, (((1,), (1,)), ((), ())), preferred_element_type=F32)


def halves(a):
    high = a.astype(BF16)
    return high, (a - high.astype(F32)).astype(BF16)


def three(product, a, b):
    a_high, a_low = halves(a)
    b_high, b_low = halves(b)
    return product(a_high, b_high) + (product(a_high, b_low) + product(a_low, b_high))


def vmem():
    return pl.BlockSpec(memory_space=pltpu.VMEM)


def params(cid):
    return pltpu.CompilerParams(collective_id=cid, has_side_effects=True, vmem_limit_bytes=VMEM_LIMIT)


def total_steps(part, slots, sum_ref, full, send, recv, again_send, again_recv):
    me = tensor_place(0)

    def scatter(j):
        return remote(part.at[tensor_place(j)], slots.at[me], send.at[j], recv.at[j], tensor_peer(j))

    def gather(j):
        return remote(sum_ref, full.at[me], again_send.at[j], again_recv.at[j], tensor_peer(j))

    for j in range(1, 16):
        scatter(j).start()
    slots[me] = part[me]
    yield
    for j in range(1, 16):
        scatter(j).wait()
    result = slots[0]
    for i in range(1, 16):
        result = result + slots[i]
    sum_ref[...] = result
    for j in range(1, 16):
        gather(j).start()
    full[me] = result
    yield
    for j in range(1, 16):
        gather(j).wait()


def total_scratch():
    sem = pltpu.SemaphoreType.DMA
    return [
        pltpu.VMEM((16, 8, 384), F32),
        pltpu.VMEM((16, 8, 384), F32),
        pltpu.VMEM((8, 384), F32),
        sem((16,)), sem((16,)), sem((16,)), sem((16,)),
    ]


def gather_steps(block, a_send, a_recv, b_send, b_recv):
    x_hi, y, core, x_lo, z = coords()
    up = place(x_hi, y, core, x_lo, (z + 1) % 8)
    down = place(x_hi, y, core, x_lo, (z + 7) % 8)
    across = place(x_hi, y, core, 1 - x_lo, z)
    own = block(x_lo, z)
    cross = remote(own, own, a_send, a_recv, across)
    cross.start()

    def copy(way, step, other):
        level = (z + 8 - step) % 8 if way == 0 else (z + step) % 8
        ref = block(1 - x_lo if other else x_lo, level)
        return remote(
            ref, ref, b_send.at[way, step, other], b_recv.at[way, step, other], up if way == 0 else down
        )

    def goes(way, step, other):
        return step < 3 or other == way

    for step in range(4):
        for other in (0, 1):
            if step == 0 and other == 1:
                cross.wait_recv()
            for way in (0, 1):
                if step > 0:
                    copy(way, step - 1, other).wait_recv()
                if goes(way, step, other):
                    copy(way, step, other).start()
        yield
    copy(0, 3, 0).wait_recv()
    copy(1, 3, 1).wait_recv()
    cross.wait_send()
    for step in range(4):
        for other in (0, 1):
            for way in (0, 1):
                if goes(way, step, other):
                    copy(way, step, other).wait_send()


def gather_scratch():
    sem = pltpu.SemaphoreType.DMA
    return [sem, sem, sem((2, 4, 2)), sem((2, 4, 2))]


def turn_peers():
    x_hi, y, core, x_lo, z = coords()
    turned = place(x_lo, (y + 4 - z // 2) % 4, core, x_hi, y * 2 + z % 2)
    turner = place(x_lo, z // 2, core, x_hi, ((z // 2 + 4 - y) % 4) * 2 + z % 2)
    stays = jnp.logical_and(x_lo == x_hi, jnp.logical_and(z // 2 == 0, y == 0))
    return turned, turner, stays


def reduce_steps(part, outbox, inbox, send, recv, xbox, xin, x_send, x_recv, tbox, tin, t_send, t_recv):
    x_hi, y, core, x_lo, z = coords()
    up = place(x_hi, y, core, x_lo, (z + 1) % 8)
    down = place(x_hi, y, core, x_lo, (z + 7) % 8)
    across = place(x_hi, y, core, 1 - x_lo, z)
    turned, turner, stays = turn_peers()

    def copy(way, step, block):
        return remote(
            outbox.at[way, step, block], inbox.at[way, step, block],
            send.at[way, step, block], recv.at[way, step, block], up if way == 0 else down,
        )

    def goes(way, step, block):
        return step > 0 or block == way

    for step in range(4):
        for block in (0, 1):
            for way in (0, 1):
                if not goes(way, step, block):
                    continue
                target = (z + 4 - step) % 8 if way == 0 else (z + 4 + step) % 8
                value = part[target, block]
                if step > 0 and goes(way, step - 1, block):
                    copy(way, step - 1, block).wait_recv()
                    value = value + inbox[way, step - 1, block].astype(F32)
                outbox[way, step, block] = value.astype(BF16)
                copy(way, step, block).start()
        yield
    for block in (0, 1):
        for way in (0, 1):
            copy(way, 3, block).wait_recv()
        part[z, block] = part[z, block] + (inbox[0, 3, block].astype(F32) + inbox[1, 3, block].astype(F32))
    xbox[...] = part[z, 1 - x_lo].astype(BF16)
    cross = remote(xbox, xin, x_send, x_recv, across)
    cross.start()
    yield
    for step in range(4):
        for block in (0, 1):
            for way in (0, 1):
                if goes(way, step, block):
                    copy(way, step, block).wait_send()
    cross.wait()
    tbox[...] = (part[z, x_lo] + xin[...].astype(F32)).astype(tbox.dtype)
    turn = remote(tbox, tin, t_send, t_recv, turned)

    @pl.when(stays)
    def _():
        tin[...] = tbox[...]

    @pl.when(jnp.logical_not(stays))
    def _():
        turn.start()

    yield

    @pl.when(jnp.logical_not(stays))
    def _():
        turn.wait()


def reduce_scratch(kind):
    sem = pltpu.SemaphoreType.DMA
    return [
        pltpu.VMEM((2, 4, 2, 128, 512), BF16),
        pltpu.VMEM((2, 4, 2, 128, 512), BF16),
        sem((2, 4, 2)), sem((2, 4, 2)),
        pltpu.VMEM((128, 512), BF16),
        pltpu.VMEM((128, 512), BF16),
        sem, sem,
        pltpu.VMEM((128, 512), kind),
        pltpu.VMEM((128, 512), kind),
        sem, sem,
    ]


def rows_first(part, result, inbox, send, recv, xin, x_send, x_recv):
    x_hi, y, core, x_lo, z = coords()
    ways = (place(x_hi, (y + 1) % 4, core, x_lo, z), place(x_hi, (y + 3) % 4, core, x_lo, z))
    across = place(1 - x_hi, y, core, x_lo, z)

    def copy(way, step, block):
        level = (y + 2) % 4 if step == 0 else (y + 1 + 2 * way) % 4
        return remote(
            part.at[block * 4 + level], inbox.at[way, step, block],
            send.at[way, step, block], recv.at[way, step, block], ways[way],
        )

    for way in (0, 1):
        copy(way, 0, way).start()
    for way in (0, 1):
        copy(way, 1, 1 - way).start()
    yield
    for way in (0, 1):
        copy(way, 0, way).wait_recv()
        level = (y + 1 + 2 * way) % 4
        part[way * 4 + level] = part[way * 4 + level] + inbox[way, 0, way]
        copy(way, 1, way).start()
    yield
    cross = remote(part.at[(1 - x_hi) * 4 + y], xin, x_send, x_recv, across)
    for block in (0, 1):
        for way in (0, 1):
            copy(way, 1, block).wait_recv()
        part[block * 4 + y] = part[block * 4 + y] + (inbox[0, 1, block] + inbox[1, 1, block])
    cross.start()
    yield
    cross.wait()
    result[...] = part[x_hi * 4 + y] + xin[...]
    for way in (0, 1):
        copy(way, 0, way).wait_send()
        for block in (0, 1):
            copy(way, 1, block).wait_send()


def rows_scratch():
    sem = pltpu.SemaphoreType.DMA
    return [
        pltpu.VMEM((2, 2, 2, 128, 512), F32),
        sem((2, 2, 2)), sem((2, 2, 2)),
        pltpu.VMEM((128, 512), F32),
        sem, sem,
    ]


def across_first(part, result, xin, x_send, x_recv, inbox, send, recv):
    x_hi, y, core, x_lo, z = coords()
    ways = (place(x_hi, (y + 1) % 4, core, x_lo, z), place(x_hi, (y + 3) % 4, core, x_lo, z))
    across = place(1 - x_hi, y, core, x_lo, z)
    far = (y + 2) % 4

    def cross(i):
        return remote(
            part.at[(1 - x_hi) * 4 + (y + i) % 4], xin.at[i], x_send.at[i], x_recv.at[i], across
        )

    def half(way):
        rows = pl.ds(64 * way, 64)
        return remote(
            part.at[x_hi * 4 + far, rows], inbox.at[way, 0, rows], send.at[way, 0], recv.at[way, 0], ways[way]
        )

    def whole(way):
        level = (y + 1 + 2 * way) % 4
        return remote(
            part.at[x_hi * 4 + level], inbox.at[way, 1], send.at[way, 1], recv.at[way, 1], ways[way]
        )

    def add(i):
        cross(i).wait_recv()
        at = x_hi * 4 + (y + i) % 4
        part[at] = part[at] + xin[i]

    for i in (2, 1, 3, 0):
        cross(i).start()
    yield
    add(2)
    for way in (0, 1):
        half(way).start()
    yield
    for way in (0, 1):
        add(1 + 2 * way)
        half(way).wait_recv()
        at = x_hi * 4 + (y + 1 + 2 * way) % 4
        rows = slice(64 * way, 64 * way + 64)
        part[at, rows, :] = part[at, rows, :] + inbox[way, 0, rows, :]
        whole(way).start()
    yield
    add(0)
    for way in (0, 1):
        whole(way).wait_recv()
    result[...] = part[x_hi * 4 + y] + (inbox[0, 1] + inbox[1, 1])
    for i in range(4):
        cross(i).wait_send()
    for way in (0, 1):
        half(way).wait_send()
        whole(way).wait_send()


def across_scratch():
    sem = pltpu.SemaphoreType.DMA
    return [
        pltpu.VMEM((4, 128, 512), F32),
        sem((4,)), sem((4,)),
        pltpu.VMEM((2, 2, 128, 512), F32),
        sem((2, 2)), sem((2, 2)),
    ]


def project_kernel(
    tok, up, wg, wv, wo, s_in, s_out, s_step,
    tokc, upc, wcat, wof, gate, value, gn, state,
    part_g, part_v, part_n, w_send, w_recv, t_send, t_recv, u_send, u_recv, *scratch,
):
    x_hi, y, core, x_lo, z = coords()
    chip = x_hi * 4 + y
    for_state, scratch = scratch[:7], scratch[7:]
    for_upstream, scratch = scratch[:4], scratch[4:]
    for_gate, scratch = scratch[:6], scratch[6:]
    for_value, for_normed = scratch[:6], scratch[6:]

    def to_chip(j):
        return ((x_hi + j // 4) % 2) * 4 + (y + j % 4) % 4

    def from_chip(j):
        return ((x_hi + j // 4) % 2) * 4 + (y + 4 - j % 4) % 4

    partner = core_peer()
    devices = [chip_peer(j) for j in range(1, 8)] + [partner] + [tensor_peer(j) for j in range(1, 16)]
    announce(devices)
    slab = tok[:, pl.ds(pl.multiple_of((x_lo * 8 + z) * 512, 512), 512)]
    state_part = for_state[0]
    for i, weights in enumerate((s_in, s_out, s_step)):
        state_part[:, :, 128 * i : 128 * i + 128] = dot(slab, weights[...]).reshape(16, 8, 128)
    gathered(len(devices))

    mine = pl.ds(pl.multiple_of(core * 512, 512), 512)
    w_copies = []
    for i, (src, dst) in enumerate(
        ((wg, wcat.at[mine, pl.ds(0, 512)]), (wv, wcat.at[mine, pl.ds(512, 512)]), (wo, wof.at[mine, :]))
    ):
        copy = remote(src, dst, w_send.at[i], w_recv.at[i], partner)
        copy.start()
        w_copies.append(copy)

    rows = pl.ds(pl.multiple_of(z * 16, 16), 16)
    side = pl.ds(pl.multiple_of(x_lo * 512, 512), 512)

    def up_copy(j):
        columns = pl.ds(pl.multiple_of(to_chip(j) * 1024 + x_lo * 512, 512), 512)
        return remote(up.at[rows, columns], upc.at[chip, rows, side], u_send.at[j], u_recv.at[j], chip_peer(j))

    def tok_copy(j):
        columns = pl.ds(pl.multiple_of(to_chip(j) * 1024, 1024), 1024)
        return remote(tok.at[:, columns], tokc.at[chip], t_send.at[j], t_recv.at[j], chip_peer(j))

    for j in range(1, 8):
        up_copy(j).start()
    state_steps = total_steps(state_part, for_state[1], for_state[2], state, *for_state[3:])
    drive(state_steps)
    for j in range(1, 8):
        tok_copy(j).start()

    wcat[mine, pl.ds(0, 512)] = wg[...]
    wcat[mine, pl.ds(512, 512)] = wv[...]
    wof[mine, :] = wo[...]
    tokc[chip] = tok[:, pl.ds(pl.multiple_of(chip * 1024, 1024), 1024)]
    upc[chip, rows, side] = up[rows, pl.ds(pl.multiple_of(chip * 1024 + x_lo * 512, 512), 512)]
    for j in range(1, 8):
        up_copy(j).wait()

    def up_block(at_side, level):
        return upc.at[
            :, pl.ds(pl.multiple_of(level * 16, 16), 16), pl.ds(pl.multiple_of(at_side * 512, 512), 512)
        ]

    up_steps = gather_steps(up_block, *for_upstream)
    drive(up_steps)
    drive(state_steps)
    for copy in w_copies:
        copy.wait()
    drive(up_steps, 2)

    def multiply(src):
        part_g[src] = dot(tokc[src], wcat[:, 0:512])
        part_v[src] = dot(tokc[src], wcat[:, 512:1024])

    multiply(chip)

    def serve(j, carry):
        tok_copy(j).wait()
        multiply(from_chip(j))
        return carry

    lax.fori_loop(1, 8, serve, 0)
    gate_steps = across_first(part_g, gate, *for_gate)
    value_steps = rows_first(part_v, value, *for_value)
    drive(value_steps)
    drive(gate_steps)
    finish(up_steps)

    def serve_upstream(src, carry):
        part_n[src] = dot(upc[src], wof[...])
        return carry

    lax.fori_loop(0, 8, serve_upstream, 0)
    normed_steps = rows_first(part_n, gn, *for_normed)
    drive(value_steps)
    drive(normed_steps)
    drive(gate_steps)
    finish(state_steps)
    drive(value_steps)
    drive(normed_steps)
    drive(gate_steps)
    drive(normed_steps)
    finish(value_steps)
    finish(gate_steps)
    finish(normed_steps)


def project(*args):
    sem = pltpu.SemaphoreType.DMA
    return pl.pallas_call(
        project_kernel,
        out_shape=(
            jax.ShapeDtypeStruct((8, 128, 1024), BF16),
            jax.ShapeDtypeStruct((8, 128, 1024), BF16),
            jax.ShapeDtypeStruct((1024, 1024), BF16),
            jax.ShapeDtypeStruct((1024, 512), BF16),
            jax.ShapeDtypeStruct((128, 512), F32),
            jax.ShapeDtypeStruct((128, 512), F32),
            jax.ShapeDtypeStruct((128, 512), F32),
            jax.ShapeDtypeStruct((16, 8, 384), F32),
        ),
        in_specs=[vmem()] * 8,
        out_specs=(vmem(),) * 8,
        scratch_shapes=[
            pltpu.VMEM((8, 128, 512), F32),
            pltpu.VMEM((8, 128, 512), F32),
            pltpu.VMEM((8, 128, 512), F32),
            sem((3,)), sem((3,)),
        ] + [sem((8,))] * 4 + total_scratch() + gather_scratch() + across_scratch() + rows_scratch() * 2,
        compiler_params=params(0),
        cost_estimate=pl.CostEstimate(flops=3 * 10**9, bytes_accessed=200 * 10**6, transcendentals=0),
        name="project",
    )(*args)


def columns_of(rows):
    pad = jnp.zeros((128 - rows.shape[0], 128), F32)
    return jnp.concatenate([rows, pad], axis=0).T


def decay_terms(raw, log, b, c):
    step = jnp.maximum(raw, 0.0) + jnp.log1p(jnp.exp(-jnp.abs(raw)))
    growth = jnp.exp(log)
    rate = growth * step
    first = lax.broadcasted_iota(jnp.int32, (128, 128), 0)
    second = lax.broadcasted_iota(jnp.int32, (128, 128), 1)
    upper = (first <= second).astype(F32)
    cumulative = jnp.dot(rate, upper, precision=HIGH, preferred_element_type=F32)
    affinity = lax.dot_general(c, b, (((1,), (1,)), ((), ())), precision=HIGH, preferred_element_type=F32)
    return raw, step, growth, rate, cumulative, affinity, first >= second


def decay_of(cumulative, cum_cols, causal, h):
    spread = jnp.where(causal, cum_cols[:, h : h + 1] - cumulative[h : h + 1, :], 0.0)
    return jnp.where(causal, jnp.exp(-spread), 0.0)


def split_pair(pair):
    lane = lax.broadcasted_iota(jnp.int32, pair.shape, 1)
    return jnp.concatenate([jnp.where(lane < 64, pair, 0.0), jnp.where(lane < 64, 0.0, pair)], axis=0)


def mix_kernel(
    gate, value, gn, state, heads, gain,
    normed, gate_low, value_low, backs, small,
    step_rows, mixed, gated, d_mixed, part, slots, send, recv,
):
    devices = [tensor_peer(j) for j in range(1, 16)]
    announce(devices)
    me = tensor_place(0)
    b = state[:, :, 0:128].reshape(128, 128)
    c = state[:, :, 128:256].reshape(128, 128)
    step_rows[...] = state[:, :, 256:384].reshape(128, 128).T
    own_heads = pl.ds(pl.multiple_of(me * 8, 8), 8)
    raw, step, growth, rate, cumulative, affinity, causal = decay_terms(
        step_rows[own_heads, :] + heads[:, 0:1], heads[:, 1:2], b, c
    )
    cum_cols = columns_of(cumulative)
    lane = lax.broadcasted_iota(jnp.int32, (128, 128), 1)
    decays = []
    for h in range(8):
        decays.append(decay_of(cumulative, cum_cols, causal, h))
    for p in range(4):
        lanes = slice(128 * p, 128 * p + 128)
        kernels = [decays[h] * affinity * step[h : h + 1, :] for h in (2 * p, 2 * p + 1)]
        pair = value[:, lanes]
        skip = jnp.where(lane < 64, heads[2 * p : 2 * p + 1, 2:3], heads[2 * p + 1 : 2 * p + 2, 2:3])
        mixed[:, lanes] = three(dot, jnp.concatenate(kernels, axis=1), split_pair(pair)) + skip * pair
    g = gate[...]
    sig = 1.0 / (1.0 + jnp.exp(-g))
    gated[...] = mixed[...] * (g * sig)
    square = jnp.sum(gated[...] * gated[...], axis=1, keepdims=True)
    inner = jnp.sum(gn[...] * gain[...] * gated[...], axis=1, keepdims=True)
    part[...] = jnp.where(lane == 0, square, jnp.where(lane == 1, inner, 0.0)).T[0:8, :]
    gathered(len(devices))

    def copy(j):
        return remote(part, slots.at[me], send.at[j], recv.at[j], tensor_peer(j))

    for j in range(1, 16):
        copy(j).start()
    slots[me] = part[...]
    for j in range(1, 16):
        copy(j).wait()
    sums = slots[0]
    for i in range(1, 16):
        sums = sums + slots[i]

    inv_row = lax.rsqrt(sums[0:1, :] * (1.0 / INNER) + EPS)
    pull_row = inv_row * inv_row * inv_row * sums[1:2, :] * (1.0 / INNER)
    token_cols = columns_of(jnp.concatenate([inv_row, pull_row, jnp.zeros((6, 128), F32)], axis=0))
    inv = token_cols[:, 0:1]
    pull = token_cols[:, 1:2]
    unit = gated[...] * inv
    normed[...] = (unit * gain[...]).astype(BF16)
    gain_sum = jnp.sum(gn[...] * unit, axis=0, keepdims=True)
    grad = inv * (gn[...] * gain[...]) - gated[...] * pull
    g = gate[...]
    sig = 1.0 / (1.0 + jnp.exp(-g))
    gate_low[...] = (grad * mixed[...] * (sig * (1.0 + g * (1.0 - sig)))).astype(BF16)
    d_mixed[...] = grad * (g * sig)
    skip_sum = jnp.sum(d_mixed[...] * value[...], axis=0, keepdims=True)
    d_affinity = jnp.zeros((128, 128), F32)
    row_sums = jnp.zeros((128, 128), F32)
    col_sums = []
    for p in range(4):
        lanes = slice(128 * p, 128 * p + 128)
        dm_pair = d_mixed[:, lanes]
        dm_split = split_pair(dm_pair)
        pair = value[:, lanes]
        d_kernel = three(dot_cols, dm_split, pair)
        kernels = []
        for i, h in enumerate((2 * p, 2 * p + 1)):
            decay = decays[h]
            step_h = step[h : h + 1, :]
            weighted = decay * d_kernel[128 * i : 128 * i + 128, :]
            d_affinity = d_affinity + weighted * step_h
            direct = weighted * affinity
            col_sums.append(jnp.sum(direct, axis=0, keepdims=True))
            row_sums = jnp.where(lane == h, jnp.sum(direct * step_h, axis=1, keepdims=True), row_sums)
            kernels.append(decay * affinity * step_h)
        skip = jnp.where(lane < 64, heads[2 * p : 2 * p + 1, 2:3], heads[2 * p + 1 : 2 * p + 2, 2:3])
        value_low[:, lanes] = (
            three(dot_rows, jnp.concatenate(kernels, axis=0), dm_split) + skip * dm_pair
        ).astype(BF16)
    direct_step = jnp.concatenate(col_sums, axis=0)
    d_cumulative = direct_step * step - row_sums.T[0:8, :]
    d_rate = jnp.dot(d_cumulative, causal.astype(F32), precision=HIGH, preferred_element_type=F32)
    d_raw = (direct_step + growth * d_rate) * (1.0 / (1.0 + jnp.exp(-raw)))
    step_rows[...] = jnp.zeros((128, 128), F32)
    step_rows[own_heads, :] = d_raw
    backs[:, 0:128] = three(dot_rows, d_affinity, c)
    backs[:, 128:256] = three(dot, d_affinity, b)
    backs[:, 256:384] = step_rows[...].T
    lane8 = lax.broadcasted_iota(jnp.int32, (8, 128), 1)
    bias_sum = jnp.sum(d_raw, axis=1, keepdims=True)
    decay_sum = jnp.sum(d_rate * rate, axis=1, keepdims=True)
    small[...] = jnp.zeros((16, 384), F32)
    small[0:1, :] = gain_sum[:, 0:384]
    small[1:2, 0:128] = gain_sum[:, 384:512]
    small[2:3, :] = skip_sum[:, 0:384]
    small[3:4, 0:128] = skip_sum[:, 384:512]
    small[8:16, 0:128] = jnp.where(lane8 == 0, bias_sum, jnp.where(lane8 == 1, decay_sum, 0.0))


def mix(*args):
    sem = pltpu.SemaphoreType.DMA
    return pl.pallas_call(
        mix_kernel,
        out_shape=(
            jax.ShapeDtypeStruct((128, 512), BF16),
            jax.ShapeDtypeStruct((128, 512), BF16),
            jax.ShapeDtypeStruct((128, 512), BF16),
            jax.ShapeDtypeStruct((128, 384), F32),
            jax.ShapeDtypeStruct((16, 384), F32),
        ),
        in_specs=[vmem()] * 6,
        out_specs=(vmem(),) * 5,
        scratch_shapes=[
            pltpu.VMEM((128, 128), F32),
            pltpu.VMEM((128, 512), F32),
            pltpu.VMEM((128, 512), F32),
            pltpu.VMEM((128, 512), F32),
            pltpu.VMEM((8, 128), F32),
            pltpu.VMEM((16, 8, 128), F32),
            sem((16,)), sem((16,)),
        ],
        compiler_params=params(1),
        name="mix",
    )(*args)


def small_steps(grads, half, total, slots, own, full, c_send, c_recv, s_send, s_recv, g_send, g_recv, e_send, e_recv):
    x_hi, y, core, x_lo, z = coords()
    chip = x_hi * 4 + y
    partner = core_peer()

    def to_chip(j):
        return ((x_hi + j // 4) % 2) * 4 + (y + j % 4) % 4

    def swap():
        return remote(grads.at[1 - core], half, c_send, c_recv, partner)

    def scatter(j):
        return remote(total.at[to_chip(j)], slots.at[chip], s_send.at[j], s_recv.at[j], chip_peer(j))

    def gather(j):
        return remote(own, full.at[core, chip], g_send.at[j], g_recv.at[j], chip_peer(j))

    def share():
        return remote(full.at[core], full.at[core], e_send, e_recv, partner)

    swap().start()
    yield
    swap().wait()
    total[...] = grads[core] + half[...]
    for j in range(1, 8):
        scatter(j).start()
    slots[chip] = total[chip]
    yield
    for j in range(1, 8):
        scatter(j).wait()
    result = slots[0]
    for i in range(1, 8):
        result = result + slots[i]
    own[...] = result
    for j in range(1, 8):
        gather(j).start()
    full[core, chip] = result
    yield
    for j in range(1, 8):
        gather(j).wait()
    share().start()
    yield
    share().wait()


def small_scratch():
    sem = pltpu.SemaphoreType.DMA
    return [
        pltpu.VMEM((2, 8, 40, 384), F32),
        pltpu.VMEM((8, 40, 384), F32),
        pltpu.VMEM((8, 40, 384), F32),
        pltpu.VMEM((8, 40, 384), F32),
        pltpu.VMEM((40, 384), F32),
        pltpu.VMEM((2, 8, 40, 384), F32),
        sem, sem, sem((8,)), sem((8,)), sem((8,)), sem((8,)), sem, sem,
    ]


def output_kernel(
    normed, gate_low, value_low, backs, small, tok, tokc, upc, wcat, wof, s_in, s_out, s_step,
    layer_out, input_grad, grad_gate, grad_value, grad_output, grad_in, grad_out, grad_step, grad_small,
    all_n, all_g, all_v, part_l, part_d, side, low, g_send, g_recv, grads, grads_in, h_send, h_recv, *scratch,
):
    x_hi, y, core, x_lo, z = coords()
    chip = x_hi * 4 + y
    for_total, scratch = scratch[:8], scratch[8:]
    for_small, scratch = scratch[:14], scratch[14:]
    for_layer, scratch = scratch[:12], scratch[12:]
    for_input, scratch = scratch[:12], scratch[12:]
    gather_layer, gather_input = scratch[:4], scratch[4:]
    partner = core_peer()
    turned, turner, stays = turn_peers()
    devices = [chip_peer(j) for j in range(1, 8)] + [partner] + [tensor_peer(j) for j in range(1, 16)]
    announce(devices)

    @pl.when(jnp.logical_not(stays))
    def _():
        announce([turned, turner])

    gathered(len(devices) + jnp.where(stays, 0, 2))
    sources = (normed, gate_low, value_low)
    targets = (all_n, all_g, all_v)

    def copy(i, j):
        return remote(sources[i], targets[i].at[chip], g_send.at[i, j], g_recv.at[i, j], chip_peer(j))

    for j in range(1, 8):
        copy(0, j).start()
    back_part, back_full = for_total[0], for_total[7]
    back_part[...] = backs[...].reshape(16, 8, 384)
    back_steps = total_steps(back_part, for_total[1], for_total[2], back_full, *for_total[3:7])
    drive(back_steps)
    for i in range(3):
        targets[i][chip] = sources[i][...]
    for j in range(1, 8):
        copy(0, j).wait_recv()
    for i in (1, 2):
        for j in range(1, 8):
            copy(i, j).start()

    def store(part, index, block):
        row = 2 * ((y + 4 - index % 4) % 4)
        part[row, index // 4] = block[:, :512]
        part[row + 1, index // 4] = block[:, 512:]

    def out_block(index, carry):
        store(part_l, index, dot_cols(all_n[index], wof[...]))
        return carry

    lax.fori_loop(0, 8, out_block, 0)
    layer_steps = reduce_steps(part_l, *for_layer)
    drive(layer_steps)
    drive(back_steps)

    theirs = pl.ds(pl.multiple_of((1 - core) * 512, 512), 512)
    mine = pl.ds(pl.multiple_of(core * 512, 512), 512)

    def grad_copy(i):
        return remote(grads.at[i, theirs], grads_in.at[i], h_send.at[i], h_recv.at[i], partner)

    def weight_grad(i, left, right):
        def rows(index, carry):
            at = pl.ds(pl.multiple_of(index * 256, 256), 256)
            grads[i, at, :] = dot_rows(left[:, :, at].reshape(1024, 256), right[...].reshape(1024, 512))
            return carry

        lax.fori_loop(0, 4, rows, 0)
        grad_copy(i).start()

    drive(layer_steps)
    weight_grad(0, upc, all_n)
    drive(layer_steps)
    finish(back_steps)
    low[...] = back_full[...].reshape(128, 384).astype(BF16)
    side[...] = (
        dot_cols(low[:, 0:128], s_in[...]) + dot_cols(low[:, 128:256], s_out[...])
        + dot_cols(low[:, 256:384], s_step[...])
    )
    slab = tok[:, pl.ds(pl.multiple_of((x_lo * 8 + z) * 512, 512), 512)]
    state_grads = jnp.concatenate(
        [dot_rows(slab, low[...]), small[...], jnp.zeros((112, 384), F32)], axis=0
    )
    for_small[0][...] = state_grads.reshape(2, 8, 40, 384)
    sum_steps = small_steps(*for_small)
    drive(sum_steps)
    drive(layer_steps)

    for i in (1, 2):
        for j in range(1, 8):
            copy(i, j).wait_recv()

    def dense_block(index, carry):
        store(
            part_d, index, dot_cols(all_g[index], wcat[:, 0:512]) + dot_cols(all_v[index], wcat[:, 512:1024])
        )
        return carry

    lax.fori_loop(0, 8, dense_block, 0)
    input_steps = reduce_steps(part_d, *for_input)
    drive(input_steps)
    drive(layer_steps)
    drive(sum_steps)
    drive(input_steps)
    drive(layer_steps)
    drive(sum_steps)
    drive(input_steps)
    finish(layer_steps)

    def blocks_of(result):
        def block(at_side, level):
            return result.at[:, pl.ds(pl.multiple_of((at_side * 8 + level) * 512, 512), 512)]

        return block

    own = pl.ds(pl.multiple_of((x_lo * 8 + z) * 512, 512), 512)
    layer_out[:, own] = for_layer[9][...]
    layer_gather = gather_steps(blocks_of(layer_out), *gather_layer)
    drive(layer_gather)
    weight_grad(1, tokc, all_g)
    drive(input_steps)
    drive(layer_gather)
    drive(sum_steps)
    drive(input_steps)
    drive(layer_gather)
    drive(input_steps)
    drive(layer_gather)
    weight_grad(2, tokc, all_v)
    finish(input_steps)
    input_grad[:, own] = (for_input[9][...] + side[...]).astype(BF16)
    input_gather = gather_steps(blocks_of(input_grad), *gather_input)
    drive(input_gather)
    finish(layer_gather)
    finish(sum_steps)
    summed = for_small[5][...].reshape(640, 384)
    grad_in[...] = summed[0:512, 0:128]
    grad_out[...] = summed[0:512, 128:256]
    grad_step[...] = summed[0:512, 256:384]
    grad_small[...] = summed[512:528, :]
    drive(input_gather)
    outs = (grad_output, grad_gate, grad_value)
    for i in range(2):
        grad_copy(i).wait_recv()
        outs[i][...] = grads[i, mine, :] + grads_in[i]
    drive(input_gather)
    grad_copy(2).wait_recv()
    grad_value[...] = grads[2, mine, :] + grads_in[2]
    finish(input_gather)
    for i in range(3):
        grad_copy(i).wait_send()
        for j in range(1, 8):
            copy(i, j).wait_send()


def outputs(*args):
    sem = pltpu.SemaphoreType.DMA
    return pl.pallas_call(
        output_kernel,
        out_shape=(
            jax.ShapeDtypeStruct((128, 8192), BF16),
            jax.ShapeDtypeStruct((128, 8192), BF16),
            jax.ShapeDtypeStruct((512, 512), F32),
            jax.ShapeDtypeStruct((512, 512), F32),
            jax.ShapeDtypeStruct((512, 512), F32),
            jax.ShapeDtypeStruct((512, 128), F32),
            jax.ShapeDtypeStruct((512, 128), F32),
            jax.ShapeDtypeStruct((512, 128), F32),
            jax.ShapeDtypeStruct((16, 384), F32),
        ),
        in_specs=[vmem()] * 13,
        out_specs=(vmem(),) * 9,
        scratch_shapes=[
            pltpu.VMEM((8, 128, 512), BF16),
            pltpu.VMEM((8, 128, 512), BF16),
            pltpu.VMEM((8, 128, 512), BF16),
            pltpu.VMEM((8, 2, 128, 512), F32),
            pltpu.VMEM((8, 2, 128, 512), F32),
            pltpu.VMEM((128, 512), F32),
            pltpu.VMEM((128, 384), BF16),
            sem((3, 8)), sem((3, 8)),
            pltpu.VMEM((3, 1024, 512), F32),
            pltpu.VMEM((3, 512, 512), F32),
            sem((3,)), sem((3,)),
        ]
        + total_scratch() + [pltpu.VMEM((16, 8, 384), F32)]
        + small_scratch() + reduce_scratch(BF16) + reduce_scratch(F32) + gather_scratch() * 2,
        compiler_params=params(2),
        cost_estimate=pl.CostEstimate(flops=6 * 10**9, bytes_accessed=300 * 10**6, transcendentals=0),
        name="outputs",
    )(*args)


def per_device(
    tokens_in, proj_gate, proj_value, state_in, state_out, proj_step,
    step_bias, decay_log, skip_scale, norm_gain, proj_output, upstream,
):
    tokc, upc, wcat, wof, gate, value, gn, state = project(
        tokens_in, upstream, proj_gate, proj_value, proj_output, state_in, state_out, proj_step
    )
    heads = jnp.pad(jnp.stack([step_bias, decay_log, skip_scale], axis=1), ((0, 0), (0, 125)))
    normed, gate_low, value_low, backs, small = mix(gate, value, gn, state, heads, norm_gain.reshape(1, 512))
    (
        layer_out, input_grad, grad_gate, grad_value, grad_output,
        grad_state_in, grad_state_out, grad_step, sums,
    ) = outputs(
        normed, gate_low, value_low, backs, small, tokens_in, tokc, upc, wcat, wof, state_in, state_out, proj_step
    )
    grad_gain = jnp.concatenate([sums[0], sums[1, :128]])
    grad_skip = jnp.concatenate([sums[2], sums[3, :128]]).reshape(8, 64).sum(axis=1)
    return (
        layer_out, input_grad, grad_gate, grad_value, grad_output,
        grad_state_in, grad_state_out, grad_step, sums[8:16, 0], sums[8:16, 1], grad_skip, grad_gain,
    )


def solution(mesh):
    block = P("dp", "tensor")
    rows = P("dp", None)
    slab = P("tensor", None)
    vector = P("tensor")
    return jax.shard_map(
        per_device,
        mesh=mesh,
        in_specs=(rows, block, block, slab, slab, slab, vector, vector, vector, vector, block, rows),
        out_specs=(rows, rows, block, block, block, slab, slab, slab, vector, vector, vector, vector),
        check_vma=False,
    )
```

```python
import jax
import jax.numpy as jnp
from jax import lax
from jax.experimental import pallas as pl
from jax.experimental.pallas import tpu as pltpu
from jax.sharding import PartitionSpec as P

MESH = pl.DeviceIdType.MESH
HIGH = lax.Precision.HIGHEST
EPS = 1e-05
INNER = 8192
F32 = jnp.float32
BF16 = jnp.bfloat16
VMEM_LIMIT = 60 * 2**20


def coords():
    d = lax.axis_index("dp")
    t = lax.axis_index("tensor")
    return d // 8, (d // 2) % 4, d % 2, t // 8, t % 8


def place(x_hi, y, core, x_lo, z):
    return (x_hi * 8 + y * 2 + core, x_lo * 8 + z)


def announce(devices):
    barrier = pltpu.get_barrier_semaphore()
    for device in devices:
        pl.semaphore_signal(barrier, inc=1, device_id=device, device_id_type=MESH)


def gathered(count):
    pl.semaphore_wait(pltpu.get_barrier_semaphore(), count)


def chip_peer(j):
    x_hi, y, core, x_lo, z = coords()
    return place((x_hi + j // 4) % 2, (y + j % 4) % 4, core, x_lo, z)


def core_peer():
    x_hi, y, core, x_lo, z = coords()
    return place(x_hi, y, 1 - core, x_lo, z)


def tensor_peer(j):
    x_hi, y, core, x_lo, z = coords()
    return place(x_hi, y, core, (x_lo + j // 8) % 2, (z + j % 8) % 8)


def tensor_place(j):
    x_hi, y, core, x_lo, z = coords()
    return ((x_lo + j // 8) % 2) * 8 + (z + j % 8) % 8


def drive(steps, count=1):
    for _ in range(count):
        next(steps, None)


def finish(steps):
    for _ in steps:
        pass


def remote(src, dst, send, recv, device):
    return pltpu.make_async_remote_copy(
        src_ref=src, dst_ref=dst, send_sem=send, recv_sem=recv, device_id=device, device_id_type=MESH
    )


def dot(a, b):
    return jnp.dot(a, b, preferred_element_type=F32)


def dot_rows(a, b):
    return lax.dot_general(a, b, (((0,), (0,)), ((), ())), preferred_element_type=F32)


def dot_cols(a, b):
    return lax.dot_general(a, b, (((1,), (1,)), ((), ())), preferred_element_type=F32)


def halves(a):
    high = a.astype(BF16)
    return high, (a - high.astype(F32)).astype(BF16)


def three(product, a, b):
    a_high, a_low = halves(a)
    b_high, b_low = halves(b)
    return product(a_high, b_high) + (product(a_high, b_low) + product(a_low, b_high))


def vmem():
    return pl.BlockSpec(memory_space=pltpu.VMEM)


def params(cid):
    return pltpu.CompilerParams(collective_id=cid, has_side_effects=True, vmem_limit_bytes=VMEM_LIMIT)


def total_steps(part, slots, sum_ref, full, send, recv, again_send, again_recv):
    me = tensor_place(0)

    def scatter(j):
        return remote(part.at[tensor_place(j)], slots.at[me], send.at[j], recv.at[j], tensor_peer(j))

    def gather(j):
        return remote(sum_ref, full.at[me], again_send.at[j], again_recv.at[j], tensor_peer(j))

    for j in range(1, 16):
        scatter(j).start()
    slots[me] = part[me]
    yield
    for j in range(1, 16):
        scatter(j).wait()
    result = slots[0]
    for i in range(1, 16):
        result = result + slots[i]
    sum_ref[...] = result
    for j in range(1, 16):
        gather(j).start()
    full[me] = result
    yield
    for j in range(1, 16):
        gather(j).wait()


def total_scratch():
    sem = pltpu.SemaphoreType.DMA
    return [
        pltpu.VMEM((16, 8, 384), F32),
        pltpu.VMEM((16, 8, 384), F32),
        pltpu.VMEM((8, 384), F32),
        sem((16,)), sem((16,)), sem((16,)), sem((16,)),
    ]


def along_z():
    x_hi, y, core, x_lo, z = coords()
    return (
        8, z, x_lo, place(x_hi, y, core, x_lo, (z + 1) % 8), place(x_hi, y, core, x_lo, (z + 7) % 8),
        place(x_hi, y, core, 1 - x_lo, z),
    )


def along_y():
    x_hi, y, core, x_lo, z = coords()
    return (
        4, y, x_hi, place(x_hi, (y + 1) % 4, core, x_lo, z), place(x_hi, (y + 3) % 4, core, x_lo, z),
        place(1 - x_hi, y, core, x_lo, z),
    )


def gather_steps(ring, block, a_send, a_recv, b_send, b_recv):
    size, here, side, up, down, across = ring
    count = size // 2
    own = block(side, here)
    cross = remote(own, own, a_send, a_recv, across)
    cross.start()

    def copy(way, step, other):
        level = (here + size - step) % size if way == 0 else (here + step) % size
        ref = block(1 - side if other else side, level)
        return remote(
            ref, ref, b_send.at[way, step, other], b_recv.at[way, step, other], up if way == 0 else down
        )

    def goes(way, step, other):
        return step < count - 1 or other == way

    for step in range(count):
        for other in (0, 1):
            if step == 0 and other == 1:
                yield
                cross.wait_recv()
            for way in (0, 1):
                if step > 0:
                    copy(way, step - 1, other).wait_recv()
                if goes(way, step, other):
                    copy(way, step, other).start()
        yield
    copy(0, count - 1, 0).wait_recv()
    copy(1, count - 1, 1).wait_recv()
    cross.wait_send()
    for step in range(count):
        for other in (0, 1):
            for way in (0, 1):
                if goes(way, step, other):
                    copy(way, step, other).wait_send()


def gather_scratch(count):
    sem = pltpu.SemaphoreType.DMA
    return [sem, sem, sem((2, count, 2)), sem((2, count, 2))]


def gather_last_across(array, d_send, d_recv, x_send, x_recv):
    x_hi, y, core, x_lo, z = coords()
    ways = (place(x_hi, (y + 1) % 4, core, x_lo, z), place(x_hi, (y + 3) % 4, core, x_lo, z))
    across = place(1 - x_hi, y, core, x_lo, z)

    def near(way):
        ref = array.at[x_hi * 4 + y]
        return remote(ref, ref, d_send.at[way, 0], d_recv.at[way, 0], ways[way])

    def far(way):
        ref = array.at[x_hi * 4 + (y + 3 + 2 * way) % 4, pl.ds(64 * way, 64)]
        return remote(ref, ref, d_send.at[way, 1], d_recv.at[way, 1], ways[way])

    def cross(i):
        ref = array.at[x_hi * 4 + (y + i) % 4]
        return remote(ref, ref, x_send.at[i], x_recv.at[i], across)

    for way in (0, 1):
        near(way).start()
    cross(0).start()
    yield
    for way in (0, 1):
        near(way).wait_recv()
        far(way).start()
        cross(3 - 2 * way).start()
    yield
    for way in (0, 1):
        far(way).wait_recv()
    cross(2).start()
    yield
    for i in range(4):
        cross(i).wait()
    for way in (0, 1):
        near(way).wait_send()
        far(way).wait_send()


def last_across_scratch():
    sem = pltpu.SemaphoreType.DMA
    return [sem((2, 2)), sem((2, 2)), sem((4,)), sem((4,))]


def turn_peers():
    x_hi, y, core, x_lo, z = coords()
    turned = place(x_lo, (y + 4 - z // 2) % 4, core, x_hi, y * 2 + z % 2)
    turner = place(x_lo, z // 2, core, x_hi, ((z // 2 + 4 - y) % 4) * 2 + z % 2)
    stays = jnp.logical_and(x_lo == x_hi, jnp.logical_and(z // 2 == 0, y == 0))
    return turned, turner, stays


def reduce_steps(part, outbox, inbox, send, recv, xbox, xin, x_send, x_recv, tbox, tin, t_send, t_recv):
    x_hi, y, core, x_lo, z = coords()
    ways = (place(x_hi, y, core, x_lo, (z + 1) % 8), place(x_hi, y, core, x_lo, (z + 7) % 8))
    across = place(x_hi, y, core, 1 - x_lo, z)
    turned, turner, stays = turn_peers()
    other = 1 - x_lo

    def level(way, distance):
        return (z + distance) % 8 if way == 0 else (z + 8 - distance) % 8

    def copy(way, i):
        at = (way, i, pl.ds(64 * way, 64)) if i == 2 else (way, i)
        return remote(outbox.at[at], inbox.at[at], send.at[way, i], recv.at[way, i], ways[way])

    def cross(i):
        return remote(xbox.at[i], xin.at[i], x_send.at[i], x_recv.at[i], across)

    def received(way, i):
        copy(way, i).wait_recv()
        return inbox[way, i].astype(F32)

    def push(way, i, value):
        outbox[way, i] = value.astype(BF16)
        copy(way, i).start()

    xbox[0] = part[(z + 4) % 8, other].astype(BF16)
    cross(0).start()
    for way in (0, 1):
        push(way, 0, part[level(way, 3), other])
    xbox[3] = part[z, other].astype(BF16)
    cross(3).start()
    yield
    cross(0).wait_recv()
    far = (part[(z + 4) % 8, x_lo] + xin[0].astype(F32)).astype(BF16)
    for way in (0, 1):
        outbox[way, 2, 64 * way : 64 * way + 64, :] = far[64 * way : 64 * way + 64, :]
        copy(way, 2).start()
    for way in (0, 1):
        push(way, 1, part[level(way, 2), other] + received(way, 0))
    yield
    for way in (0, 1):
        copy(way, 2).wait_recv()
        rows = slice(64 * way, 64 * way + 64)
        at = level(way, 3)
        part[at, x_lo, rows, :] = part[at, x_lo, rows, :] + inbox[way, 2, rows, :].astype(F32)
        push(way, 3, part[at, x_lo])
    for way in (0, 1):
        xbox[1 + way] = (part[level(way, 1), other] + received(way, 1)).astype(BF16)
        cross(1 + way).start()
    yield
    for way in (0, 1):
        push(way, 4, part[level(way, 2), x_lo] + received(way, 3))
    yield
    for way in (0, 1):
        cross(1 + way).wait_recv()
        push(way, 5, part[level(way, 1), x_lo] + xin[1 + way].astype(F32) + received(way, 4))
    yield
    cross(3).wait_recv()
    home = part[z, x_lo] + xin[3].astype(F32)
    tbox[...] = (home + (received(0, 5) + received(1, 5))).astype(tbox.dtype)
    turn = remote(tbox, tin, t_send, t_recv, turned)

    @pl.when(stays)
    def _():
        tin[...] = tbox[...]

    @pl.when(jnp.logical_not(stays))
    def _():
        turn.start()

    for way in (0, 1):
        for i in range(6):
            copy(way, i).wait_send()
    for i in range(4):
        cross(i).wait_send()
    yield

    @pl.when(jnp.logical_not(stays))
    def _():
        turn.wait()


def reduce_scratch(kind):
    sem = pltpu.SemaphoreType.DMA
    return [
        pltpu.VMEM((2, 6, 128, 512), BF16),
        pltpu.VMEM((2, 6, 128, 512), BF16),
        sem((2, 6)), sem((2, 6)),
        pltpu.VMEM((4, 128, 512), BF16),
        pltpu.VMEM((4, 128, 512), BF16),
        sem((4,)), sem((4,)),
        pltpu.VMEM((128, 512), kind),
        pltpu.VMEM((128, 512), kind),
        sem, sem,
    ]


def spread_steps(block, z_send, z_recv, x_send, x_recv):
    x_hi, y, core, x_lo, z = coords()
    ways = (place(x_hi, y, core, x_lo, (z + 1) % 8), place(x_hi, y, core, x_lo, (z + 7) % 8))
    across = place(x_hi, y, core, 1 - x_lo, z)

    def level(way, distance):
        return (z + 8 - distance) % 8 if way == 0 else (z + distance) % 8

    def copy(way, i):
        if i < 3:
            ref = block(x_lo, level(way, i), None)
        elif i == 3:
            ref = block(x_lo, level(way, 3), way)
        else:
            ref = block(1 - x_lo, level(way, i - 3), None)
        return remote(ref, ref, z_send.at[way, i], z_recv.at[way, i], ways[way])

    def cross(i):
        ref = block(x_lo, (z, level(0, 1), level(1, 1), (z + 4) % 8)[i], None)
        return remote(ref, ref, x_send.at[i], x_recv.at[i], across)

    for way in (0, 1):
        copy(way, 0).start()
    cross(0).start()
    yield
    for way in (0, 1):
        copy(way, 0).wait_recv()
        copy(way, 1).start()
        cross(1 + way).start()
    yield
    for way in (0, 1):
        copy(way, 1).wait_recv()
        copy(way, 2).start()
    for way in (0, 1):
        cross(1 + way).wait_recv()
        copy(way, 4).start()
    yield
    for way in (0, 1):
        copy(way, 2).wait_recv()
        copy(way, 3).start()
    for way in (0, 1):
        copy(way, 4).wait_recv()
        copy(way, 5).start()
    yield
    for way in (0, 1):
        copy(way, 3).wait_recv()
    cross(3).start()
    yield
    for way in (0, 1):
        copy(way, 5).wait_recv()
    cross(0).wait_recv()
    cross(3).wait_recv()
    for way in (0, 1):
        for i in range(6):
            copy(way, i).wait_send()
    for i in range(4):
        cross(i).wait_send()


def spread_scratch():
    sem = pltpu.SemaphoreType.DMA
    return [sem((2, 6)), sem((2, 6)), sem((4,)), sem((4,))]


def rows_first(part, result, inbox, send, recv, xin, x_send, x_recv):
    x_hi, y, core, x_lo, z = coords()
    ways = (place(x_hi, (y + 1) % 4, core, x_lo, z), place(x_hi, (y + 3) % 4, core, x_lo, z))
    across = place(1 - x_hi, y, core, x_lo, z)

    def copy(way, step, block):
        level = (y + 2) % 4 if step == 0 else (y + 1 + 2 * way) % 4
        return remote(
            part.at[block * 4 + level], inbox.at[way, step, block],
            send.at[way, step, block], recv.at[way, step, block], ways[way],
        )

    for way in (0, 1):
        copy(way, 0, way).start()
    for way in (0, 1):
        copy(way, 1, 1 - way).start()
    yield
    for way in (0, 1):
        copy(way, 0, way).wait_recv()
        level = (y + 1 + 2 * way) % 4
        part[way * 4 + level] = part[way * 4 + level] + inbox[way, 0, way]
        copy(way, 1, way).start()
    yield
    cross = remote(part.at[(1 - x_hi) * 4 + y], xin, x_send, x_recv, across)
    for block in (0, 1):
        for way in (0, 1):
            copy(way, 1, block).wait_recv()
        part[block * 4 + y] = part[block * 4 + y] + (inbox[0, 1, block] + inbox[1, 1, block])
    cross.start()
    yield
    cross.wait()
    result[...] = part[x_hi * 4 + y] + xin[...]
    for way in (0, 1):
        copy(way, 0, way).wait_send()
        for block in (0, 1):
            copy(way, 1, block).wait_send()


def rows_scratch():
    sem = pltpu.SemaphoreType.DMA
    return [
        pltpu.VMEM((2, 2, 2, 128, 512), F32),
        sem((2, 2, 2)), sem((2, 2, 2)),
        pltpu.VMEM((128, 512), F32),
        sem, sem,
    ]


def across_first(part, result, xin, x_send, x_recv, inbox, send, recv):
    x_hi, y, core, x_lo, z = coords()
    ways = (place(x_hi, (y + 1) % 4, core, x_lo, z), place(x_hi, (y + 3) % 4, core, x_lo, z))
    across = place(1 - x_hi, y, core, x_lo, z)
    far = (y + 2) % 4

    def cross(i):
        return remote(
            part.at[(1 - x_hi) * 4 + (y + i) % 4], xin.at[i], x_send.at[i], x_recv.at[i], across
        )

    def half(way):
        rows = pl.ds(64 * way, 64)
        return remote(
            part.at[x_hi * 4 + far, rows], inbox.at[way, 0, rows], send.at[way, 0], recv.at[way, 0], ways[way]
        )

    def whole(way):
        level = (y + 1 + 2 * way) % 4
        return remote(
            part.at[x_hi * 4 + level], inbox.at[way, 1], send.at[way, 1], recv.at[way, 1], ways[way]
        )

    def add(i):
        cross(i).wait_recv()
        at = x_hi * 4 + (y + i) % 4
        part[at] = part[at] + xin[i]

    for i in (2, 1, 3, 0):
        cross(i).start()
    yield
    add(2)
    for way in (0, 1):
        half(way).start()
    yield
    for way in (0, 1):
        add(1 + 2 * way)
        half(way).wait_recv()
        at = x_hi * 4 + (y + 1 + 2 * way) % 4
        rows = slice(64 * way, 64 * way + 64)
        part[at, rows, :] = part[at, rows, :] + inbox[way, 0, rows, :]
        whole(way).start()
    yield
    add(0)
    for way in (0, 1):
        whole(way).wait_recv()
    result[...] = part[x_hi * 4 + y] + (inbox[0, 1] + inbox[1, 1])
    for i in range(4):
        cross(i).wait_send()
    for way in (0, 1):
        half(way).wait_send()
        whole(way).wait_send()


def across_scratch():
    sem = pltpu.SemaphoreType.DMA
    return [
        pltpu.VMEM((4, 128, 512), F32),
        sem((4,)), sem((4,)),
        pltpu.VMEM((2, 2, 128, 512), F32),
        sem((2, 2)), sem((2, 2)),
    ]


def project_kernel(
    tok, up, wg, wv, wo, s_in, s_out, s_step,
    tokc, upc, wcat, wof, gate, value, gn, state, slab_out,
    part_g, part_v, part_n, w_send, w_recv, p_send, p_recv, f_send, f_recv, *scratch,
):
    x_hi, y, core, x_lo, z = coords()
    chip = x_hi * 4 + y
    for_state, scratch = scratch[:7], scratch[7:]
    for_tokens, scratch = scratch[:4], scratch[4:]
    for_upstream, scratch = scratch[:4], scratch[4:]
    for_gate, scratch = scratch[:6], scratch[6:]
    for_value, for_normed = scratch[:6], scratch[6:]

    def to_chip(j):
        return ((x_hi + j // 4) % 2) * 4 + (y + j % 4) % 4

    def from_chip(j):
        return ((x_hi + j // 4) % 2) * 4 + (y + 4 - j % 4) % 4

    partner = core_peer()
    devices = [chip_peer(j) for j in range(1, 8)] + [partner] + [tensor_peer(j) for j in range(1, 16)]
    announce(devices)
    gathered(len(devices))
    mine = pl.ds(pl.multiple_of(core * 512, 512), 512)

    rows = pl.ds(pl.multiple_of(z * 16, 16), 16)
    side = pl.ds(pl.multiple_of(512 + x_lo * 256, 256), 256)
    direct = pl.ds(0, 512)
    sources, arrays = (tok, up), (tokc, upc)

    def part_copy(i, j):
        columns = pl.ds(pl.multiple_of(to_chip(j) * 1024 + 512 + x_lo * 256, 256), 256)
        return remote(
            sources[i].at[rows, columns], arrays[i].at[chip, rows, side], p_send.at[i, j], p_recv.at[i, j], chip_peer(j)
        )

    def full_copy(i, j):
        columns = pl.ds(pl.multiple_of(to_chip(j) * 1024, 1024), 512)
        return remote(
            sources[i].at[:, columns], arrays[i].at[chip, :, direct], f_send.at[i, j], f_recv.at[i, j], chip_peer(j)
        )

    def keep(i):
        arrays[i][chip, :, direct] = sources[i][:, pl.ds(pl.multiple_of(chip * 1024, 1024), 512)]
        own = pl.ds(pl.multiple_of(chip * 1024 + 512 + x_lo * 256, 256), 256)
        arrays[i][chip, rows, side] = sources[i][rows, own]

    def shared(array):
        def block(at_side, level):
            columns = pl.ds(pl.multiple_of(512 + at_side * 256, 256), 256)
            return array.at[:, pl.ds(pl.multiple_of(level * 16, 16), 16), columns]

        return block

    for j in range(1, 8):
        part_copy(0, j).start()
    for j in range(1, 8):
        full_copy(0, j).start()
    keep(0)
    w_copies = []
    for i, (src, dst) in enumerate(
        ((wg, wcat.at[mine, pl.ds(0, 512)]), (wv, wcat.at[mine, pl.ds(512, 512)]), (wo, wof.at[mine, :]))
    ):
        copy = remote(src, dst, w_send.at[i], w_recv.at[i], partner)
        copy.start()
        w_copies.append(copy)
    for j in range(1, 8):
        part_copy(0, j).wait()
    tok_steps = gather_steps(along_z(), shared(tokc), *for_tokens)
    drive(tok_steps)
    for j in range(1, 8):
        part_copy(1, j).start()
    slab = tok[:, pl.ds(pl.multiple_of((x_lo * 8 + z) * 512, 512), 512)]
    slab_out[...] = slab
    state_part = for_state[0]
    for i, weights in enumerate((s_in, s_out, s_step)):
        state_part[:, :, 128 * i : 128 * i + 128] = dot(slab, weights[...]).reshape(16, 8, 128)
    drive(tok_steps)
    keep(1)
    wcat[mine, pl.ds(0, 512)] = wg[...]
    wcat[mine, pl.ds(512, 512)] = wv[...]
    wof[mine, :] = wo[...]
    drive(tok_steps)
    for j in range(1, 8):
        part_copy(1, j).wait()
    drive(tok_steps)
    for j in range(1, 8):
        full_copy(1, j).start()
    up_steps = gather_steps(along_z(), shared(upc), *for_upstream)
    drive(up_steps)
    for copy in w_copies:
        copy.wait()
    drive(tok_steps)
    finish(tok_steps)
    drive(up_steps)
    for j in range(1, 8):
        full_copy(0, j).wait()

    def multiply(part, tokens, weights, start):
        def columns(n, carry):
            at = pl.ds(pl.multiple_of(n * 256, 256), 256)
            weight = weights[:, pl.ds(pl.multiple_of(start + n * 256, 256), 256)]
            part[:, :, at] = dot(tokens[...].reshape(1024, 1024), weight).reshape(8, 128, 256)
            return carry

        lax.fori_loop(0, 2, columns, 0)

    gate_steps = across_first(part_g, gate, *for_gate)
    value_steps = rows_first(part_v, value, *for_value)
    normed_steps = rows_first(part_n, gn, *for_normed)
    multiply(part_g, tokc, wcat, 0)
    drive(gate_steps)
    multiply(part_v, tokc, wcat, 512)
    drive(value_steps)
    drive(up_steps)
    state_steps = total_steps(state_part, for_state[1], for_state[2], state, *for_state[3:])
    drive(state_steps)
    drive(up_steps)
    drive(value_steps)
    drive(up_steps)
    finish(up_steps)
    for j in range(1, 8):
        full_copy(1, j).wait()
    multiply(part_n, upc, wof, 0)
    drive(normed_steps)
    drive(gate_steps)
    drive(state_steps)
    drive(normed_steps)
    drive(gate_steps)
    drive(value_steps)
    drive(gate_steps)
    finish(state_steps)
    drive(normed_steps)
    finish(value_steps)
    finish(gate_steps)
    finish(normed_steps)


def project(*args):
    sem = pltpu.SemaphoreType.DMA
    return pl.pallas_call(
        project_kernel,
        out_shape=(
            jax.ShapeDtypeStruct((8, 128, 1024), BF16),
            jax.ShapeDtypeStruct((8, 128, 1024), BF16),
            jax.ShapeDtypeStruct((1024, 1024), BF16),
            jax.ShapeDtypeStruct((1024, 512), BF16),
            jax.ShapeDtypeStruct((128, 512), F32),
            jax.ShapeDtypeStruct((128, 512), F32),
            jax.ShapeDtypeStruct((128, 512), F32),
            jax.ShapeDtypeStruct((16, 8, 384), F32),
            jax.ShapeDtypeStruct((128, 512), BF16),
        ),
        in_specs=[vmem()] * 8,
        out_specs=(vmem(),) * 9,
        scratch_shapes=[
            pltpu.VMEM((8, 128, 512), F32),
            pltpu.VMEM((8, 128, 512), F32),
            pltpu.VMEM((8, 128, 512), F32),
            sem((3,)), sem((3,)),
        ] + [sem((2, 8))] * 4 + total_scratch() + gather_scratch(4) * 2 + across_scratch() + rows_scratch() * 2,
        compiler_params=params(0),
        cost_estimate=pl.CostEstimate(flops=3 * 10**9, bytes_accessed=200 * 10**6, transcendentals=0),
        name="project",
    )(*args)


def columns_of(rows):
    pad = jnp.zeros((128 - rows.shape[0], 128), F32)
    return jnp.concatenate([rows, pad], axis=0).T


def decay_terms(raw, log, b, c):
    step = jnp.maximum(raw, 0.0) + jnp.log1p(jnp.exp(-jnp.abs(raw)))
    growth = jnp.exp(log)
    rate = growth * step
    first = lax.broadcasted_iota(jnp.int32, (128, 128), 0)
    second = lax.broadcasted_iota(jnp.int32, (128, 128), 1)
    upper = (first <= second).astype(F32)
    cumulative = jnp.dot(rate, upper, precision=HIGH, preferred_element_type=F32)
    affinity = lax.dot_general(c, b, (((1,), (1,)), ((), ())), precision=HIGH, preferred_element_type=F32)
    return raw, step, growth, rate, cumulative, affinity, first >= second


def decay_of(cumulative, cum_cols, causal, h):
    spread = jnp.where(causal, cum_cols[:, h : h + 1] - cumulative[h : h + 1, :], 0.0)
    return jnp.where(causal, jnp.exp(-spread), 0.0)


def split_pair(pair):
    lane = lax.broadcasted_iota(jnp.int32, pair.shape, 1)
    return jnp.concatenate([jnp.where(lane < 64, pair, 0.0), jnp.where(lane < 64, 0.0, pair)], axis=0)


def mix_steps(
    gate, value, gn, state, heads, gain, normed, gate_low, value_low, backs, small,
    step_rows, mixed, gated, d_mixed, part, slots, send, recv,
):
    me = tensor_place(0)
    b = state[:, :, 0:128].reshape(128, 128)
    c = state[:, :, 128:256].reshape(128, 128)
    step_rows[...] = state[:, :, 256:384].reshape(128, 128).T
    own_heads = pl.ds(pl.multiple_of(me * 8, 8), 8)
    raw, step, growth, rate, cumulative, affinity, causal = decay_terms(
        step_rows[own_heads, :] + heads[:, 0:1], heads[:, 1:2], b, c
    )
    cum_cols = columns_of(cumulative)
    lane = lax.broadcasted_iota(jnp.int32, (128, 128), 1)
    decays = []
    for h in range(8):
        decays.append(decay_of(cumulative, cum_cols, causal, h))
    for p in range(4):
        lanes = slice(128 * p, 128 * p + 128)
        kernels = [decays[h] * affinity * step[h : h + 1, :] for h in (2 * p, 2 * p + 1)]
        pair = value[:, lanes]
        skip = jnp.where(lane < 64, heads[2 * p : 2 * p + 1, 2:3], heads[2 * p + 1 : 2 * p + 2, 2:3])
        mixed[:, lanes] = three(dot, jnp.concatenate(kernels, axis=1), split_pair(pair)) + skip * pair
    g = gate[...]
    sig = 1.0 / (1.0 + jnp.exp(-g))
    gated[...] = mixed[...] * (g * sig)
    square = jnp.sum(gated[...] * gated[...], axis=1, keepdims=True)
    inner = jnp.sum(gn[...] * gain[...] * gated[...], axis=1, keepdims=True)
    part[...] = jnp.where(lane == 0, square, jnp.where(lane == 1, inner, 0.0)).T[0:8, :]
    yield

    def copy(j):
        return remote(part, slots.at[me], send.at[j], recv.at[j], tensor_peer(j))

    for j in range(1, 16):
        copy(j).start()
    slots[me] = part[...]
    yield
    for j in range(1, 16):
        copy(j).wait()
    sums = slots[0]
    for i in range(1, 16):
        sums = sums + slots[i]

    inv_row = lax.rsqrt(sums[0:1, :] * (1.0 / INNER) + EPS)
    pull_row = inv_row * inv_row * inv_row * sums[1:2, :] * (1.0 / INNER)
    token_cols = columns_of(jnp.concatenate([inv_row, pull_row, jnp.zeros((6, 128), F32)], axis=0))
    inv = token_cols[:, 0:1]
    pull = token_cols[:, 1:2]
    unit = gated[...] * inv
    normed[...] = (unit * gain[...]).astype(BF16)
    yield
    gain_sum = jnp.sum(gn[...] * unit, axis=0, keepdims=True)
    grad = inv * (gn[...] * gain[...]) - gated[...] * pull
    g = gate[...]
    sig = 1.0 / (1.0 + jnp.exp(-g))
    gate_low[...] = (grad * mixed[...] * (sig * (1.0 + g * (1.0 - sig)))).astype(BF16)
    d_mixed[...] = grad * (g * sig)
    skip_sum = jnp.sum(d_mixed[...] * value[...], axis=0, keepdims=True)
    d_affinity = jnp.zeros((128, 128), F32)
    row_sums = jnp.zeros((128, 128), F32)
    col_sums = []
    for p in range(4):
        lanes = slice(128 * p, 128 * p + 128)
        dm_pair = d_mixed[:, lanes]
        dm_split = split_pair(dm_pair)
        pair = value[:, lanes]
        d_kernel = three(dot_cols, dm_split, pair)
        kernels = []
        for i, h in enumerate((2 * p, 2 * p + 1)):
            decay = decays[h]
            step_h = step[h : h + 1, :]
            weighted = decay * d_kernel[128 * i : 128 * i + 128, :]
            d_affinity = d_affinity + weighted * step_h
            direct = weighted * affinity
            col_sums.append(jnp.sum(direct, axis=0, keepdims=True))
            row_sums = jnp.where(lane == h, jnp.sum(direct * step_h, axis=1, keepdims=True), row_sums)
            kernels.append(decay * affinity * step_h)
        skip = jnp.where(lane < 64, heads[2 * p : 2 * p + 1, 2:3], heads[2 * p + 1 : 2 * p + 2, 2:3])
        value_low[:, lanes] = (
            three(dot_rows, jnp.concatenate(kernels, axis=0), dm_split) + skip * dm_pair
        ).astype(BF16)
    direct_step = jnp.concatenate(col_sums, axis=0)
    d_cumulative = direct_step * step - row_sums.T[0:8, :]
    d_rate = jnp.dot(d_cumulative, causal.astype(F32), precision=HIGH, preferred_element_type=F32)
    d_raw = (direct_step + growth * d_rate) * (1.0 / (1.0 + jnp.exp(-raw)))
    step_rows[...] = jnp.zeros((128, 128), F32)
    step_rows[own_heads, :] = d_raw
    backs[:, 0:128] = three(dot_rows, d_affinity, c)
    backs[:, 128:256] = three(dot, d_affinity, b)
    backs[:, 256:384] = step_rows[...].T
    lane8 = lax.broadcasted_iota(jnp.int32, (8, 128), 1)
    bias_sum = jnp.sum(d_raw, axis=1, keepdims=True)
    decay_sum = jnp.sum(d_rate * rate, axis=1, keepdims=True)
    small[...] = jnp.zeros((16, 384), F32)
    small[0:1, :] = gain_sum[:, 0:384]
    small[1:2, 0:128] = gain_sum[:, 384:512]
    small[2:3, :] = skip_sum[:, 0:384]
    small[3:4, 0:128] = skip_sum[:, 384:512]
    small[8:16, 0:128] = jnp.where(lane8 == 0, bias_sum, jnp.where(lane8 == 1, decay_sum, 0.0))


def mix_scratch():
    sem = pltpu.SemaphoreType.DMA
    return [
        pltpu.VMEM((128, 512), BF16),
        pltpu.VMEM((128, 512), BF16),
        pltpu.VMEM((128, 512), BF16),
        pltpu.VMEM((128, 384), F32),
        pltpu.VMEM((16, 384), F32),
        pltpu.VMEM((128, 128), F32),
        pltpu.VMEM((128, 512), F32),
        pltpu.VMEM((128, 512), F32),
        pltpu.VMEM((128, 512), F32),
        pltpu.VMEM((8, 128), F32),
        pltpu.VMEM((16, 8, 128), F32),
        sem((16,)), sem((16,)),
    ]


def small_steps(grads, half, total, slots, own, full, c_send, c_recv, s_send, s_recv, g_send, g_recv, e_send, e_recv):
    x_hi, y, core, x_lo, z = coords()
    chip = x_hi * 4 + y
    partner = core_peer()

    def to_chip(j):
        return ((x_hi + j // 4) % 2) * 4 + (y + j % 4) % 4

    def swap():
        return remote(grads.at[1 - core], half, c_send, c_recv, partner)

    def scatter(j):
        return remote(total.at[to_chip(j)], slots.at[chip], s_send.at[j], s_recv.at[j], chip_peer(j))

    def gather(j):
        return remote(own, full.at[core, chip], g_send.at[j], g_recv.at[j], chip_peer(j))

    def share():
        return remote(full.at[core], full.at[core], e_send, e_recv, partner)

    swap().start()
    yield
    swap().wait()
    total[...] = grads[core] + half[...]
    for j in range(1, 8):
        scatter(j).start()
    slots[chip] = total[chip]
    yield
    for j in range(1, 8):
        scatter(j).wait()
    result = slots[0]
    for i in range(1, 8):
        result = result + slots[i]
    own[...] = result
    for j in range(1, 8):
        gather(j).start()
    full[core, chip] = result
    yield
    for j in range(1, 8):
        gather(j).wait()
    share().start()
    yield
    share().wait()


def small_scratch():
    sem = pltpu.SemaphoreType.DMA
    return [
        pltpu.VMEM((2, 8, 40, 384), F32),
        pltpu.VMEM((8, 40, 384), F32),
        pltpu.VMEM((8, 40, 384), F32),
        pltpu.VMEM((8, 40, 384), F32),
        pltpu.VMEM((40, 384), F32),
        pltpu.VMEM((2, 8, 40, 384), F32),
        sem, sem, sem((8,)), sem((8,)), sem((8,)), sem((8,)), sem, sem,
    ]


def output_kernel(
    gate, value, gn, state, heads, gain, slab, s_in, s_out, s_step, tokc_far, upc_far, wcat_far, wof_far,
    layer_out, input_grad, grad_gate, grad_value, grad_output, grad_in, grad_out, grad_step, grad_small,
    all_n, all_g, all_v, part_l, part_d, side, low, grads, grads_in, h_send, h_recv,
    tokc, upc, wcat, wof, loaded, tok_t, up_t, *scratch,
):
    x_hi, y, core, x_lo, z = coords()
    chip = x_hi * 4 + y
    for_mix, scratch = scratch[:13], scratch[13:]
    normed, gate_low, value_low, backs, small = for_mix[:5]
    for_total, scratch = scratch[:8], scratch[8:]
    for_small, scratch = scratch[:14], scratch[14:]
    for_layer, scratch = scratch[:12], scratch[12:]
    for_input, scratch = scratch[:12], scratch[12:]
    gather_layer, gather_input, scratch = scratch[:4], scratch[4:8], scratch[8:]
    for_n, for_g, for_v = scratch[:4], scratch[4:8], scratch[8:]
    partner = core_peer()
    turned, turner, stays = turn_peers()
    devices = [chip_peer(j) for j in range(1, 8)] + [partner] + [tensor_peer(j) for j in range(1, 16)]
    announce(devices)

    @pl.when(jnp.logical_not(stays))
    def _():
        announce([turned, turner])

    loads = [
        pltpu.make_async_copy(source, target, loaded.at[i])
        for i, (source, target) in enumerate(((tokc_far, tokc), (upc_far, upc), (wof_far, wof), (wcat_far, wcat)))
    ]
    for load in loads:
        load.start()
    mixing = mix_steps(gate, value, gn, state, heads, gain, *for_mix)
    drive(mixing)
    gathered(len(devices) + jnp.where(stays, 0, 2))
    drive(mixing)

    def turn_over(array, target):
        def columns(index, carry):
            at = pl.ds(pl.multiple_of(index * 256, 256), 256)
            target[at, :] = array[:, :, at].reshape(1024, 256).T
            return carry

        lax.fori_loop(0, 4, columns, 0)

    loads[0].wait()
    turn_over(tokc, tok_t)
    drive(mixing)
    all_n[chip] = normed[...]

    def chips_of(array):
        return lambda at_side, level: array.at[at_side * 4 + level]

    n_steps = gather_steps(along_y(), chips_of(all_n), *for_n)
    g_steps = gather_steps(along_y(), chips_of(all_g), *for_g)
    v_steps = gather_last_across(all_v, *for_v)
    drive(n_steps)
    finish(mixing)
    all_g[chip] = gate_low[...]
    all_v[chip] = value_low[...]
    drive(g_steps)
    drive(v_steps)
    drive(n_steps)
    back_part, back_full = for_total[0], for_total[7]
    back_part[...] = backs[...].reshape(16, 8, 384)
    back_steps = total_steps(back_part, for_total[1], for_total[2], back_full, *for_total[3:7])
    drive(back_steps)
    drive(g_steps)
    loads[1].wait()
    turn_over(upc, up_t)
    drive(v_steps)
    drive(n_steps)
    drive(g_steps)
    drive(v_steps)
    finish(n_steps)
    loads[2].wait()
    loads[3].wait()

    def store(part, n, block):
        for index in range(8):
            row = 2 * ((y + 4 - index % 4) % 4) + n // 2
            at = pl.ds(pl.multiple_of((n % 2) * 256, 256), 256)
            part[row, index // 4, :, at] = block[128 * index : 128 * index + 128, :]

    def weight_rows(n):
        return pl.ds(pl.multiple_of(n * 256, 256), 256)

    def out_block(n, carry):
        store(part_l, n, dot_cols(all_n[...].reshape(1024, 512), wof[weight_rows(n), :]))
        return carry

    lax.fori_loop(0, 4, out_block, 0)
    layer_steps = reduce_steps(part_l, *for_layer)
    drive(layer_steps)
    drive(back_steps)
    finish(g_steps)
    finish(v_steps)

    def dense_block(n, carry):
        store(
            part_d, n,
            dot_cols(all_g[...].reshape(1024, 512), wcat[weight_rows(n), 0:512])
            + dot_cols(all_v[...].reshape(1024, 512), wcat[weight_rows(n), 512:1024]),
        )
        return carry

    lax.fori_loop(0, 4, dense_block, 0)
    input_steps = reduce_steps(part_d, *for_input)
    drive(input_steps)
    drive(layer_steps, 2)

    theirs = pl.ds(pl.multiple_of((1 - core) * 512, 512), 512)
    mine = pl.ds(pl.multiple_of(core * 512, 512), 512)

    def grad_copy(i):
        return remote(grads.at[i, theirs], grads_in.at[i], h_send.at[i], h_recv.at[i], partner)

    def weight_grad(i, left, right):
        def rows(half):
            def block(index, carry):
                at = pl.ds(pl.multiple_of(half * 512 + index * 256, 256), 256)
                grads[i, at, :] = dot(left[at, :], right[...].reshape(1024, 512))
                return carry

            lax.fori_loop(0, 2, block, 0)

        rows(1 - core)
        grad_copy(i).start()
        rows(core)

    finish(back_steps)
    low[...] = back_full[...].reshape(128, 384).astype(BF16)
    side[...] = (
        dot_cols(low[:, 0:128], s_in[...]) + dot_cols(low[:, 128:256], s_out[...])
        + dot_cols(low[:, 256:384], s_step[...])
    )
    state_grads = jnp.concatenate(
        [dot_rows(slab[...], low[...]), small[...], jnp.zeros((112, 384), F32)], axis=0
    )
    for_small[0][...] = state_grads.reshape(2, 8, 40, 384)
    sum_steps = small_steps(*for_small)
    drive(sum_steps)
    drive(layer_steps)
    drive(input_steps)
    drive(sum_steps)
    drive(layer_steps)
    weight_grad(0, up_t, all_n)
    drive(input_steps)
    drive(layer_steps)
    drive(sum_steps)
    drive(input_steps)
    finish(layer_steps)

    def blocks_of(result):
        def block(at_side, level, half):
            columns = pl.ds(pl.multiple_of((at_side * 8 + level) * 512, 512), 512)
            return result.at[:, columns] if half is None else result.at[pl.ds(64 * half, 64), columns]

        return block

    own = pl.ds(pl.multiple_of((x_lo * 8 + z) * 512, 512), 512)
    layer_out[:, own] = for_layer[9][...]
    layer_gather = spread_steps(blocks_of(layer_out), *gather_layer)
    drive(layer_gather)
    drive(input_steps)
    drive(sum_steps)
    drive(layer_gather)
    drive(input_steps)
    weight_grad(1, tok_t, all_g)
    drive(layer_gather)
    finish(input_steps)
    input_grad[:, own] = (for_input[9][...] + side[...]).astype(BF16)
    input_gather = spread_steps(blocks_of(input_grad), *gather_input)
    drive(input_gather)
    drive(layer_gather)
    weight_grad(2, tok_t, all_v)
    drive(input_gather)
    drive(layer_gather)
    finish(layer_gather)
    finish(sum_steps)
    summed = for_small[5][...].reshape(640, 384)
    grad_in[...] = summed[0:512, 0:128]
    grad_out[...] = summed[0:512, 128:256]
    grad_step[...] = summed[0:512, 256:384]
    grad_small[...] = summed[512:528, :]
    drive(input_gather)
    outs = (grad_output, grad_gate, grad_value)
    for i in range(3):
        grad_copy(i).wait_recv()
        outs[i][...] = grads[i, mine, :] + grads_in[i]
    drive(input_gather, 2)
    finish(input_gather)
    for i in range(3):
        grad_copy(i).wait_send()


def outputs(*args):
    sem = pltpu.SemaphoreType.DMA
    return pl.pallas_call(
        output_kernel,
        out_shape=(
            jax.ShapeDtypeStruct((128, 8192), BF16),
            jax.ShapeDtypeStruct((128, 8192), BF16),
            jax.ShapeDtypeStruct((512, 512), F32),
            jax.ShapeDtypeStruct((512, 512), F32),
            jax.ShapeDtypeStruct((512, 512), F32),
            jax.ShapeDtypeStruct((512, 128), F32),
            jax.ShapeDtypeStruct((512, 128), F32),
            jax.ShapeDtypeStruct((512, 128), F32),
            jax.ShapeDtypeStruct((16, 384), F32),
        ),
        in_specs=[vmem()] * 10 + [pl.BlockSpec(memory_space=pl.ANY)] * 4,
        out_specs=(vmem(),) * 9,
        scratch_shapes=[
            pltpu.VMEM((8, 128, 512), BF16),
            pltpu.VMEM((8, 128, 512), BF16),
            pltpu.VMEM((8, 128, 512), BF16),
            pltpu.VMEM((8, 2, 128, 512), F32),
            pltpu.VMEM((8, 2, 128, 512), F32),
            pltpu.VMEM((128, 512), F32),
            pltpu.VMEM((128, 384), BF16),
            pltpu.VMEM((3, 1024, 512), F32),
            pltpu.VMEM((3, 512, 512), F32),
            sem((3,)), sem((3,)),
            pltpu.VMEM((8, 128, 1024), BF16),
            pltpu.VMEM((8, 128, 1024), BF16),
            pltpu.VMEM((1024, 1024), BF16),
            pltpu.VMEM((1024, 512), BF16),
            sem((4,)),
            pltpu.VMEM((1024, 1024), BF16),
            pltpu.VMEM((1024, 1024), BF16),
        ]
        + mix_scratch() + total_scratch() + [pltpu.VMEM((16, 8, 384), F32)]
        + small_scratch() + reduce_scratch(BF16) + reduce_scratch(F32) + spread_scratch() * 2
        + gather_scratch(2) * 2 + last_across_scratch(),
        compiler_params=params(2),
        cost_estimate=pl.CostEstimate(flops=6 * 10**9, bytes_accessed=300 * 10**6, transcendentals=0),
        name="outputs",
    )(*args)


def settle_kernel(*refs):
    count = (len(refs) - 2) // 3
    ins, outs, boxes = refs[:count], refs[count : 2 * count], refs[2 * count : 3 * count]
    in_sems, out_sems = refs[-2:]
    loads = [pltpu.make_async_copy(ins[i], boxes[i], in_sems.at[i]) for i in range(count)]
    stores = [pltpu.make_async_copy(boxes[i], outs[i], out_sems.at[i]) for i in range(count)]
    for load in loads:
        load.start()
    for load, store in zip(loads, stores):
        load.wait()
        store.start()
    for store in stores:
        store.wait()


def settle(*arrays):
    anywhere = pl.BlockSpec(memory_space=pl.ANY)
    sem = pltpu.SemaphoreType.DMA
    return pl.pallas_call(
        settle_kernel,
        out_shape=tuple(jax.ShapeDtypeStruct(a.shape, a.dtype) for a in arrays),
        in_specs=[anywhere] * len(arrays),
        out_specs=(anywhere,) * len(arrays),
        scratch_shapes=[pltpu.VMEM(a.shape, a.dtype) for a in arrays] + [sem((len(arrays),)), sem((len(arrays),))],
        compiler_params=pltpu.CompilerParams(vmem_limit_bytes=VMEM_LIMIT),
        name="settle",
    )(*arrays)


def per_device(
    tokens_in, proj_gate, proj_value, state_in, state_out, proj_step,
    step_bias, decay_log, skip_scale, norm_gain, proj_output, upstream,
):
    tokc, upc, wcat, wof, gate, value, gn, state, slab = project(
        tokens_in, upstream, proj_gate, proj_value, proj_output, state_in, state_out, proj_step
    )
    heads = jnp.pad(jnp.stack([step_bias, decay_log, skip_scale], axis=1), ((0, 0), (0, 125)))
    *results, sums = outputs(
        gate, value, gn, state, heads, norm_gain.reshape(1, 512), slab, state_in, state_out, proj_step,
        tokc, upc, wcat, wof,
    )
    (
        layer_out, input_grad, grad_gate, grad_value, grad_output, grad_state_in, grad_state_out, grad_step,
    ) = settle(*results)
    grad_gain = jnp.concatenate([sums[0], sums[1, :128]])
    grad_skip = jnp.concatenate([sums[2], sums[3, :128]]).reshape(8, 64).sum(axis=1)
    return (
        layer_out, input_grad, grad_gate, grad_value, grad_output,
        grad_state_in, grad_state_out, grad_step, sums[8:16, 0], sums[8:16, 1], grad_skip, grad_gain,
    )


def solution(mesh):
    block = P("dp", "tensor")
    rows = P("dp", None)
    slab = P("tensor", None)
    vector = P("tensor")
    return jax.shard_map(
        per_device,
        mesh=mesh,
        in_specs=(rows, block, block, slab, slab, slab, vector, vector, vector, vector, block, rows),
        out_specs=(rows, rows, block, block, block, slab, slab, slab, vector, vector, vector, vector),
        check_vma=False,
    )
```

```python
import jax
import jax.numpy as jnp
from jax import lax
from jax.experimental import pallas as pl
from jax.experimental.pallas import tpu as pltpu
from jax.sharding import PartitionSpec as P

MESH = pl.DeviceIdType.MESH
HIGH = lax.Precision.HIGHEST
EPS = 1e-05
INNER = 8192
F32 = jnp.float32
BF16 = jnp.bfloat16
VMEM_LIMIT = 60 * 2**20
ORDER = "DL1BDLSD2LDSlGDSGDGdHGHGgsHwHH"


def coords():
    d = lax.axis_index("dp")
    t = lax.axis_index("tensor")
    return d // 8, (d // 2) % 4, d % 2, t // 8, t % 8


def place(x_hi, y, core, x_lo, z):
    return (x_hi * 8 + y * 2 + core, x_lo * 8 + z)


def announce(devices):
    barrier = pltpu.get_barrier_semaphore()
    for device in devices:
        pl.semaphore_signal(barrier, inc=1, device_id=device, device_id_type=MESH)


def gathered(count):
    pl.semaphore_wait(pltpu.get_barrier_semaphore(), count)


def chip_peer(j):
    x_hi, y, core, x_lo, z = coords()
    return place((x_hi + j // 4) % 2, (y + j % 4) % 4, core, x_lo, z)


def core_peer():
    x_hi, y, core, x_lo, z = coords()
    return place(x_hi, y, 1 - core, x_lo, z)


def tensor_peer(j):
    x_hi, y, core, x_lo, z = coords()
    return place(x_hi, y, core, (x_lo + j // 8) % 2, (z + j % 8) % 8)


def tensor_place(j):
    x_hi, y, core, x_lo, z = coords()
    return ((x_lo + j // 8) % 2) * 8 + (z + j % 8) % 8


def drive(steps, count=1):
    for _ in range(count):
        next(steps, None)


def finish(steps):
    for _ in steps:
        pass


def remote(src, dst, send, recv, device):
    return pltpu.make_async_remote_copy(
        src_ref=src, dst_ref=dst, send_sem=send, recv_sem=recv, device_id=device, device_id_type=MESH
    )


def dot(a, b):
    return jnp.dot(a, b, preferred_element_type=F32)


def dot_rows(a, b):
    return lax.dot_general(a, b, (((0,), (0,)), ((), ())), preferred_element_type=F32)


def dot_cols(a, b):
    return lax.dot_general(a, b, (((1,), (1,)), ((), ())), preferred_element_type=F32)


def halves(a):
    high = a.astype(BF16)
    return high, (a - high.astype(F32)).astype(BF16)


def three(product, a, b):
    a_high, a_low = halves(a)
    b_high, b_low = halves(b)
    return product(a_high, b_high) + (product(a_high, b_low) + product(a_low, b_high))


def vmem():
    return pl.BlockSpec(memory_space=pltpu.VMEM)


def params(cid):
    return pltpu.CompilerParams(collective_id=cid, has_side_effects=True, vmem_limit_bytes=VMEM_LIMIT)


def total_steps(part, slots, sum_ref, full, send, recv, again_send, again_recv):
    me = tensor_place(0)

    def scatter(j):
        return remote(part.at[tensor_place(j)], slots.at[me], send.at[j], recv.at[j], tensor_peer(j))

    def gather(j):
        return remote(sum_ref, full.at[me], again_send.at[j], again_recv.at[j], tensor_peer(j))

    for j in range(1, 16):
        scatter(j).start()
    slots[me] = part[me]
    yield
    for j in range(1, 16):
        scatter(j).wait()
    result = slots[0]
    for i in range(1, 16):
        result = result + slots[i]
    sum_ref[...] = result
    for j in range(1, 16):
        gather(j).start()
    full[me] = result
    yield
    for j in range(1, 16):
        gather(j).wait()


def total_scratch():
    sem = pltpu.SemaphoreType.DMA
    return [
        pltpu.VMEM((16, 8, 384), F32),
        pltpu.VMEM((16, 8, 384), F32),
        pltpu.VMEM((8, 384), F32),
        sem((16,)), sem((16,)), sem((16,)), sem((16,)),
    ]


def along_z():
    x_hi, y, core, x_lo, z = coords()
    return (
        8, z, x_lo, place(x_hi, y, core, x_lo, (z + 1) % 8), place(x_hi, y, core, x_lo, (z + 7) % 8),
        place(x_hi, y, core, 1 - x_lo, z),
    )


def along_y():
    x_hi, y, core, x_lo, z = coords()
    return (
        4, y, x_hi, place(x_hi, (y + 1) % 4, core, x_lo, z), place(x_hi, (y + 3) % 4, core, x_lo, z),
        place(1 - x_hi, y, core, x_lo, z),
    )


def gather_steps(ring, block, a_send, a_recv, b_send, b_recv):
    size, here, side, up, down, across = ring
    count = size // 2
    own = block(side, here)
    cross = remote(own, own, a_send, a_recv, across)
    cross.start()

    def copy(way, step, other):
        level = (here + size - step) % size if way == 0 else (here + step) % size
        ref = block(1 - side if other else side, level)
        return remote(
            ref, ref, b_send.at[way, step, other], b_recv.at[way, step, other], up if way == 0 else down
        )

    def goes(way, step, other):
        return step < count - 1 or other == way

    for step in range(count):
        for other in (0, 1):
            if step == 0 and other == 1:
                yield
                cross.wait_recv()
            for way in (0, 1):
                if step > 0:
                    copy(way, step - 1, other).wait_recv()
                if goes(way, step, other):
                    copy(way, step, other).start()
        yield
    copy(0, count - 1, 0).wait_recv()
    copy(1, count - 1, 1).wait_recv()
    cross.wait_send()
    for step in range(count):
        for other in (0, 1):
            for way in (0, 1):
                if goes(way, step, other):
                    copy(way, step, other).wait_send()


def gather_scratch(count):
    sem = pltpu.SemaphoreType.DMA
    return [sem, sem, sem((2, count, 2)), sem((2, count, 2))]


def turn_peers():
    x_hi, y, core, x_lo, z = coords()
    turned = place(x_lo, (y + 4 - z // 2) % 4, core, x_hi, y * 2 + z % 2)
    turner = place(x_lo, z // 2, core, x_hi, ((z // 2 + 4 - y) % 4) * 2 + z % 2)
    stays = jnp.logical_and(x_lo == x_hi, jnp.logical_and(z // 2 == 0, y == 0))
    return turned, turner, stays


def reduce_steps(part, outbox, inbox, send, recv, xbox, xin, x_send, x_recv, tbox, tin, t_send, t_recv):
    x_hi, y, core, x_lo, z = coords()
    ways = (place(x_hi, y, core, x_lo, (z + 1) % 8), place(x_hi, y, core, x_lo, (z + 7) % 8))
    across = place(x_hi, y, core, 1 - x_lo, z)
    turned, turner, stays = turn_peers()
    other = 1 - x_lo

    def level(way, distance):
        return (z + distance) % 8 if way == 0 else (z + 8 - distance) % 8

    def copy(way, i):
        at = (way, i, pl.ds(64 * way, 64)) if i == 2 else (way, i)
        return remote(outbox.at[at], inbox.at[at], send.at[way, i], recv.at[way, i], ways[way])

    def cross(i):
        return remote(xbox.at[i], xin.at[i], x_send.at[i], x_recv.at[i], across)

    def received(way, i):
        copy(way, i).wait_recv()
        return inbox[way, i].astype(F32)

    def push(way, i, value):
        outbox[way, i] = value.astype(BF16)
        copy(way, i).start()

    xbox[0] = part[(z + 4) % 8, other].astype(BF16)
    cross(0).start()
    for way in (0, 1):
        push(way, 0, part[level(way, 3), other])
    xbox[3] = part[z, other].astype(BF16)
    cross(3).start()
    yield
    cross(0).wait_recv()
    far = (part[(z + 4) % 8, x_lo] + xin[0].astype(F32)).astype(BF16)
    for way in (0, 1):
        outbox[way, 2, 64 * way : 64 * way + 64, :] = far[64 * way : 64 * way + 64, :]
        copy(way, 2).start()
    for way in (0, 1):
        push(way, 1, part[level(way, 2), other] + received(way, 0))
    yield
    for way in (0, 1):
        copy(way, 2).wait_recv()
        rows = slice(64 * way, 64 * way + 64)
        at = level(way, 3)
        part[at, x_lo, rows, :] = part[at, x_lo, rows, :] + inbox[way, 2, rows, :].astype(F32)
        push(way, 3, part[at, x_lo])
    for way in (0, 1):
        xbox[1 + way] = (part[level(way, 1), other] + received(way, 1)).astype(BF16)
        cross(1 + way).start()
    yield
    for way in (0, 1):
        push(way, 4, part[level(way, 2), x_lo] + received(way, 3))
    yield
    for way in (0, 1):
        cross(1 + way).wait_recv()
        push(way, 5, part[level(way, 1), x_lo] + xin[1 + way].astype(F32) + received(way, 4))
    yield
    cross(3).wait_recv()
    home = part[z, x_lo] + xin[3].astype(F32)
    tbox[...] = (home + (received(0, 5) + received(1, 5))).astype(tbox.dtype)
    turn = remote(tbox, tin, t_send, t_recv, turned)

    @pl.when(stays)
    def _():
        tin[...] = tbox[...]

    @pl.when(jnp.logical_not(stays))
    def _():
        turn.start()

    for way in (0, 1):
        for i in range(6):
            copy(way, i).wait_send()
    for i in range(4):
        cross(i).wait_send()
    yield

    @pl.when(jnp.logical_not(stays))
    def _():
        turn.wait()


def reduce_scratch(kind):
    sem = pltpu.SemaphoreType.DMA
    return [
        pltpu.VMEM((2, 6, 128, 512), BF16),
        pltpu.VMEM((2, 6, 128, 512), BF16),
        sem((2, 6)), sem((2, 6)),
        pltpu.VMEM((4, 128, 512), BF16),
        pltpu.VMEM((4, 128, 512), BF16),
        sem((4,)), sem((4,)),
        pltpu.VMEM((128, 512), kind),
        pltpu.VMEM((128, 512), kind),
        sem, sem,
    ]


def spread_steps(block, z_send, z_recv, x_send, x_recv):
    x_hi, y, core, x_lo, z = coords()
    ways = (place(x_hi, y, core, x_lo, (z + 1) % 8), place(x_hi, y, core, x_lo, (z + 7) % 8))
    across = place(x_hi, y, core, 1 - x_lo, z)

    def level(way, distance):
        return (z + 8 - distance) % 8 if way == 0 else (z + distance) % 8

    def copy(way, i):
        if i < 3:
            ref = block(x_lo, level(way, i), None)
        elif i == 3:
            ref = block(x_lo, level(way, 3), way)
        else:
            ref = block(1 - x_lo, level(way, i - 3), None)
        return remote(ref, ref, z_send.at[way, i], z_recv.at[way, i], ways[way])

    def cross(i):
        ref = block(x_lo, (z, level(0, 1), level(1, 1), (z + 4) % 8)[i], None)
        return remote(ref, ref, x_send.at[i], x_recv.at[i], across)

    for way in (0, 1):
        copy(way, 0).start()
    cross(0).start()
    yield
    for way in (0, 1):
        copy(way, 0).wait_recv()
        copy(way, 1).start()
        cross(1 + way).start()
    yield
    for way in (0, 1):
        copy(way, 1).wait_recv()
        copy(way, 2).start()
    for way in (0, 1):
        cross(1 + way).wait_recv()
        copy(way, 4).start()
    yield
    for way in (0, 1):
        copy(way, 2).wait_recv()
        copy(way, 3).start()
    for way in (0, 1):
        copy(way, 4).wait_recv()
        copy(way, 5).start()
    yield
    for way in (0, 1):
        copy(way, 3).wait_recv()
    cross(3).start()
    yield
    for way in (0, 1):
        copy(way, 5).wait_recv()
    cross(0).wait_recv()
    cross(3).wait_recv()
    for way in (0, 1):
        for i in range(6):
            copy(way, i).wait_send()
    for i in range(4):
        cross(i).wait_send()


def spread_scratch():
    sem = pltpu.SemaphoreType.DMA
    return [sem((2, 6)), sem((2, 6)), sem((4,)), sem((4,))]


def rows_first(part, result, outbox, inbox, send, recv, xin, x_send, x_recv):
    x_hi, y, core, x_lo, z = coords()
    ways = (place(x_hi, (y + 1) % 4, core, x_lo, z), place(x_hi, (y + 3) % 4, core, x_lo, z))
    across = place(1 - x_hi, y, core, x_lo, z)

    def copy(way, step, block):
        level = (y + 2) % 4 if step == 0 else (y + 1 + 2 * way) % 4
        source = part.at[block * 4 + level] if outbox is None else outbox.at[way, step, block]
        return remote(
            source, inbox.at[way, step, block], send.at[way, step, block], recv.at[way, step, block], ways[way]
        )

    def push(way, step, block):
        level = (y + 2) % 4 if step == 0 else (y + 1 + 2 * way) % 4
        if outbox is not None:
            outbox[way, step, block] = part[block * 4 + level].astype(outbox.dtype)
        copy(way, step, block).start()

    for way in (0, 1):
        push(way, 0, way)
    for way in (0, 1):
        push(way, 1, 1 - way)
    yield
    for way in (0, 1):
        copy(way, 0, way).wait_recv()
        level = (y + 1 + 2 * way) % 4
        part[way * 4 + level] = part[way * 4 + level] + inbox[way, 0, way].astype(F32)
        push(way, 1, way)
    yield
    cross = remote(part.at[(1 - x_hi) * 4 + y], xin, x_send, x_recv, across)
    for block in (0, 1):
        for way in (0, 1):
            copy(way, 1, block).wait_recv()
        part[block * 4 + y] = part[block * 4 + y] + (
            inbox[0, 1, block].astype(F32) + inbox[1, 1, block].astype(F32)
        )
    cross.start()
    yield
    cross.wait()
    result[...] = part[x_hi * 4 + y] + xin[...]
    for way in (0, 1):
        copy(way, 0, way).wait_send()
        for block in (0, 1):
            copy(way, 1, block).wait_send()


def rows_scratch(kind):
    sem = pltpu.SemaphoreType.DMA
    out = pltpu.VMEM((2, 2, 2, 128, 512), kind)
    boxes = [out] if kind == F32 else [out, out]
    return boxes + [sem((2, 2, 2)), sem((2, 2, 2)), pltpu.VMEM((128, 512), F32), sem, sem]


def across_first(part, result, xin, x_send, x_recv, inbox, send, recv):
    x_hi, y, core, x_lo, z = coords()
    ways = (place(x_hi, (y + 1) % 4, core, x_lo, z), place(x_hi, (y + 3) % 4, core, x_lo, z))
    across = place(1 - x_hi, y, core, x_lo, z)
    far = (y + 2) % 4

    def cross(i):
        return remote(
            part.at[(1 - x_hi) * 4 + (y + i) % 4], xin.at[i], x_send.at[i], x_recv.at[i], across
        )

    def half(way):
        rows = pl.ds(64 * way, 64)
        return remote(
            part.at[x_hi * 4 + far, rows], inbox.at[way, 0, rows], send.at[way, 0], recv.at[way, 0], ways[way]
        )

    def whole(way):
        level = (y + 1 + 2 * way) % 4
        return remote(
            part.at[x_hi * 4 + level], inbox.at[way, 1], send.at[way, 1], recv.at[way, 1], ways[way]
        )

    def add(i):
        cross(i).wait_recv()
        at = x_hi * 4 + (y + i) % 4
        part[at] = part[at] + xin[i]

    for i in (2, 1, 3, 0):
        cross(i).start()
    yield
    add(2)
    for way in (0, 1):
        half(way).start()
    yield
    for way in (0, 1):
        add(1 + 2 * way)
        half(way).wait_recv()
        at = x_hi * 4 + (y + 1 + 2 * way) % 4
        rows = slice(64 * way, 64 * way + 64)
        part[at, rows, :] = part[at, rows, :] + inbox[way, 0, rows, :]
        whole(way).start()
    yield
    add(0)
    for way in (0, 1):
        whole(way).wait_recv()
    result[...] = part[x_hi * 4 + y] + (inbox[0, 1] + inbox[1, 1])
    for i in range(4):
        cross(i).wait_send()
    for way in (0, 1):
        half(way).wait_send()
        whole(way).wait_send()


def across_scratch():
    sem = pltpu.SemaphoreType.DMA
    return [
        pltpu.VMEM((4, 128, 512), F32),
        sem((4,)), sem((4,)),
        pltpu.VMEM((2, 2, 128, 512), F32),
        sem((2, 2)), sem((2, 2)),
    ]


def project_kernel(
    tok, up, wg, wv, wo, s_in, s_out, s_step,
    tokc_far, upc_far, wcat_far, wof_far, slab_far, gate, value, gn, state,
    tokc, upc, wcat, wof, slab_out, part_g, part_v, part_n, w_send, w_recv, p_send, p_recv, f_send, f_recv, *scratch,
):
    x_hi, y, core, x_lo, z = coords()
    chip = x_hi * 4 + y
    for_state, scratch = scratch[:7], scratch[7:]
    for_tokens, scratch = scratch[:4], scratch[4:]
    for_upstream, scratch = scratch[:4], scratch[4:]
    for_gate, scratch = scratch[:6], scratch[6:]
    for_value, scratch = scratch[:6], scratch[6:]
    for_normed, stored = scratch[:7], scratch[7]

    def to_chip(j):
        return ((x_hi + j // 4) % 2) * 4 + (y + j % 4) % 4

    def from_chip(j):
        return ((x_hi + j // 4) % 2) * 4 + (y + 4 - j % 4) % 4

    partner = core_peer()
    devices = [chip_peer(j) for j in range(1, 8)] + [partner] + [tensor_peer(j) for j in range(1, 16)]
    announce(devices)
    gathered(len(devices))
    mine = pl.ds(pl.multiple_of(core * 512, 512), 512)

    rows = pl.ds(pl.multiple_of(z * 16, 16), 16)
    side = pl.ds(pl.multiple_of(512 + x_lo * 256, 256), 256)
    direct = pl.ds(0, 512)
    sources, arrays = (tok, up), (tokc, upc)

    def part_copy(i, j):
        columns = pl.ds(pl.multiple_of(to_chip(j) * 1024 + 512 + x_lo * 256, 256), 256)
        return remote(
            sources[i].at[rows, columns], arrays[i].at[chip, rows, side], p_send.at[i, j], p_recv.at[i, j], chip_peer(j)
        )

    def full_copy(i, j):
        columns = pl.ds(pl.multiple_of(to_chip(j) * 1024, 1024), 512)
        return remote(
            sources[i].at[:, columns], arrays[i].at[chip, :, direct], f_send.at[i, j], f_recv.at[i, j], chip_peer(j)
        )

    def keep(i):
        arrays[i][chip, :, direct] = sources[i][:, pl.ds(pl.multiple_of(chip * 1024, 1024), 512)]
        own = pl.ds(pl.multiple_of(chip * 1024 + 512 + x_lo * 256, 256), 256)
        arrays[i][chip, rows, side] = sources[i][rows, own]

    def shared(array):
        def block(at_side, level):
            columns = pl.ds(pl.multiple_of(512 + at_side * 256, 256), 256)
            return array.at[:, pl.ds(pl.multiple_of(level * 16, 16), 16), columns]

        return block

    for j in range(1, 8):
        part_copy(0, j).start()
    for j in range(1, 8):
        full_copy(0, j).start()
    keep(0)
    w_copies = []
    for i, (src, dst) in enumerate(
        ((wg, wcat.at[mine, pl.ds(0, 512)]), (wv, wcat.at[mine, pl.ds(512, 512)]), (wo, wof.at[mine, :]))
    ):
        copy = remote(src, dst, w_send.at[i], w_recv.at[i], partner)
        copy.start()
        w_copies.append(copy)
    for j in range(1, 8):
        part_copy(0, j).wait()
    tok_steps = gather_steps(along_z(), shared(tokc), *for_tokens)
    drive(tok_steps)
    for j in range(1, 8):
        part_copy(1, j).start()
    slab = tok[:, pl.ds(pl.multiple_of((x_lo * 8 + z) * 512, 512), 512)]
    slab_out[...] = slab
    state_part = for_state[0]
    for i, weights in enumerate((s_in, s_out, s_step)):
        state_part[:, :, 128 * i : 128 * i + 128] = dot(slab, weights[...]).reshape(16, 8, 128)
    drive(tok_steps)
    keep(1)
    wcat[mine, pl.ds(0, 512)] = wg[...]
    wcat[mine, pl.ds(512, 512)] = wv[...]
    wof[mine, :] = wo[...]
    drive(tok_steps)
    for j in range(1, 8):
        part_copy(1, j).wait()
    drive(tok_steps)
    for j in range(1, 8):
        full_copy(1, j).start()
    up_steps = gather_steps(along_z(), shared(upc), *for_upstream)
    drive(up_steps)
    for copy in w_copies:
        copy.wait()
    drive(tok_steps)
    finish(tok_steps)
    drive(up_steps)
    for j in range(1, 8):
        full_copy(0, j).wait()

    def multiply(part, tokens, weights, start):
        def columns(n, carry):
            at = pl.ds(pl.multiple_of(n * 256, 256), 256)
            weight = weights[:, pl.ds(pl.multiple_of(start + n * 256, 256), 256)]
            part[:, :, at] = dot(tokens[...].reshape(1024, 1024), weight).reshape(8, 128, 256)
            return carry

        lax.fori_loop(0, 2, columns, 0)

    gate_steps = across_first(part_g, gate, *for_gate)
    value_steps = rows_first(part_v, value, None, *for_value)
    normed_steps = rows_first(part_n, gn, *for_normed)
    stores = [
        pltpu.make_async_copy(source, target, stored.at[i])
        for i, (source, target) in enumerate(
            ((tokc, tokc_far), (wcat, wcat_far), (wof, wof_far), (slab_out, slab_far), (upc, upc_far))
        )
    ]
    multiply(part_g, tokc, wcat, 0)
    drive(gate_steps)
    multiply(part_v, tokc, wcat, 512)
    drive(value_steps)
    drive(up_steps)
    state_steps = total_steps(state_part, for_state[1], for_state[2], state, *for_state[3:])
    drive(state_steps)
    drive(up_steps)
    drive(value_steps)
    drive(up_steps)
    finish(up_steps)
    for j in range(1, 8):
        full_copy(1, j).wait()
    multiply(part_n, upc, wof, 0)
    drive(normed_steps)
    for store in stores:
        store.start()
    drive(gate_steps)
    drive(state_steps)
    drive(normed_steps)
    drive(gate_steps)
    drive(value_steps)
    drive(gate_steps)
    finish(state_steps)
    drive(normed_steps)
    finish(value_steps)
    finish(gate_steps)
    finish(normed_steps)
    for store in stores:
        store.wait()


def project(*args):
    sem = pltpu.SemaphoreType.DMA
    return pl.pallas_call(
        project_kernel,
        out_shape=(
            jax.ShapeDtypeStruct((8, 128, 1024), BF16),
            jax.ShapeDtypeStruct((8, 128, 1024), BF16),
            jax.ShapeDtypeStruct((1024, 1024), BF16),
            jax.ShapeDtypeStruct((1024, 512), BF16),
            jax.ShapeDtypeStruct((128, 512), BF16),
            jax.ShapeDtypeStruct((128, 512), F32),
            jax.ShapeDtypeStruct((128, 512), F32),
            jax.ShapeDtypeStruct((128, 512), F32),
            jax.ShapeDtypeStruct((16, 8, 384), F32),
        ),
        in_specs=[vmem()] * 8,
        out_specs=(pl.BlockSpec(memory_space=pl.ANY),) * 5 + (vmem(),) * 4,
        scratch_shapes=[
            pltpu.VMEM((8, 128, 1024), BF16),
            pltpu.VMEM((8, 128, 1024), BF16),
            pltpu.VMEM((1024, 1024), BF16),
            pltpu.VMEM((1024, 512), BF16),
            pltpu.VMEM((128, 512), BF16),
            pltpu.VMEM((8, 128, 512), F32),
            pltpu.VMEM((8, 128, 512), F32),
            pltpu.VMEM((8, 128, 512), F32),
            sem((3,)), sem((3,)),
        ] + [sem((2, 8))] * 4 + total_scratch() + gather_scratch(4) * 2 + across_scratch() + rows_scratch(F32) + rows_scratch(BF16) + [sem((5,))],
        compiler_params=params(0),
        cost_estimate=pl.CostEstimate(flops=3 * 10**9, bytes_accessed=200 * 10**6, transcendentals=0),
        name="project",
    )(*args)


def columns_of(rows):
    pad = jnp.zeros((128 - rows.shape[0], 128), F32)
    return jnp.concatenate([rows, pad], axis=0).T


def decay_terms(raw, log, b, c):
    step = jnp.maximum(raw, 0.0) + jnp.log1p(jnp.exp(-jnp.abs(raw)))
    growth = jnp.exp(log)
    rate = growth * step
    first = lax.broadcasted_iota(jnp.int32, (128, 128), 0)
    second = lax.broadcasted_iota(jnp.int32, (128, 128), 1)
    upper = (first <= second).astype(F32)
    cumulative = jnp.dot(rate, upper, precision=HIGH, preferred_element_type=F32)
    affinity = lax.dot_general(c, b, (((1,), (1,)), ((), ())), precision=HIGH, preferred_element_type=F32)
    return raw, step, growth, rate, cumulative, affinity, first >= second


def decay_of(cumulative, cum_cols, causal, h):
    spread = jnp.where(causal, cum_cols[:, h : h + 1] - cumulative[h : h + 1, :], 0.0)
    return jnp.where(causal, jnp.exp(-spread), 0.0)


def split_pair(pair):
    lane = lax.broadcasted_iota(jnp.int32, pair.shape, 1)
    return jnp.concatenate([jnp.where(lane < 64, pair, 0.0), jnp.where(lane < 64, 0.0, pair)], axis=0)


def mix_steps(
    gate, value, gn, state, heads, gain, normed, gate_low, value_low, backs, small,
    step_rows, mixed, gated, d_mixed, part, slots, send, recv,
):
    me = tensor_place(0)
    b = state[:, :, 0:128].reshape(128, 128)
    c = state[:, :, 128:256].reshape(128, 128)
    step_rows[...] = state[:, :, 256:384].reshape(128, 128).T
    own_heads = pl.ds(pl.multiple_of(me * 8, 8), 8)
    raw, step, growth, rate, cumulative, affinity, causal = decay_terms(
        step_rows[own_heads, :] + heads[:, 0:1], heads[:, 1:2], b, c
    )
    cum_cols = columns_of(cumulative)
    lane = lax.broadcasted_iota(jnp.int32, (128, 128), 1)
    decays = []
    for h in range(8):
        decays.append(decay_of(cumulative, cum_cols, causal, h))
    for p in range(4):
        lanes = slice(128 * p, 128 * p + 128)
        kernels = [decays[h] * affinity * step[h : h + 1, :] for h in (2 * p, 2 * p + 1)]
        pair = value[:, lanes]
        skip = jnp.where(lane < 64, heads[2 * p : 2 * p + 1, 2:3], heads[2 * p + 1 : 2 * p + 2, 2:3])
        mixed[:, lanes] = three(dot, jnp.concatenate(kernels, axis=1), split_pair(pair)) + skip * pair
    g = gate[...]
    sig = 1.0 / (1.0 + jnp.exp(-g))
    gated[...] = mixed[...] * (g * sig)
    square = jnp.sum(gated[...] * gated[...], axis=1, keepdims=True)
    inner = jnp.sum(gn[...] * gain[...] * gated[...], axis=1, keepdims=True)
    part[...] = jnp.where(lane == 0, square, jnp.where(lane == 1, inner, 0.0)).T[0:8, :]
    yield

    def copy(j):
        return remote(part, slots.at[me], send.at[j], recv.at[j], tensor_peer(j))

    for j in range(1, 16):
        copy(j).start()
    slots[me] = part[...]
    yield
    for j in range(1, 16):
        copy(j).wait()
    sums = slots[0]
    for i in range(1, 16):
        sums = sums + slots[i]

    inv_row = lax.rsqrt(sums[0:1, :] * (1.0 / INNER) + EPS)
    pull_row = inv_row * inv_row * inv_row * sums[1:2, :] * (1.0 / INNER)
    token_cols = columns_of(jnp.concatenate([inv_row, pull_row, jnp.zeros((6, 128), F32)], axis=0))
    inv = token_cols[:, 0:1]
    pull = token_cols[:, 1:2]
    unit = gated[...] * inv
    normed[...] = (unit * gain[...]).astype(BF16)
    yield
    gain_sum = jnp.sum(gn[...] * unit, axis=0, keepdims=True)
    grad = inv * (gn[...] * gain[...]) - gated[...] * pull
    g = gate[...]
    sig = 1.0 / (1.0 + jnp.exp(-g))
    gate_low[...] = (grad * mixed[...] * (sig * (1.0 + g * (1.0 - sig)))).astype(BF16)
    d_mixed[...] = grad * (g * sig)
    skip_sum = jnp.sum(d_mixed[...] * value[...], axis=0, keepdims=True)
    d_affinity = jnp.zeros((128, 128), F32)
    row_sums = jnp.zeros((128, 128), F32)
    col_sums = []
    for p in range(4):
        lanes = slice(128 * p, 128 * p + 128)
        dm_pair = d_mixed[:, lanes]
        dm_split = split_pair(dm_pair)
        pair = value[:, lanes]
        d_kernel = three(dot_cols, dm_split, pair)
        kernels = []
        for i, h in enumerate((2 * p, 2 * p + 1)):
            decay = decays[h]
            step_h = step[h : h + 1, :]
            weighted = decay * d_kernel[128 * i : 128 * i + 128, :]
            d_affinity = d_affinity + weighted * step_h
            direct = weighted * affinity
            col_sums.append(jnp.sum(direct, axis=0, keepdims=True))
            row_sums = jnp.where(lane == h, jnp.sum(direct * step_h, axis=1, keepdims=True), row_sums)
            kernels.append(decay * affinity * step_h)
        skip = jnp.where(lane < 64, heads[2 * p : 2 * p + 1, 2:3], heads[2 * p + 1 : 2 * p + 2, 2:3])
        value_low[:, lanes] = (
            three(dot_rows, jnp.concatenate(kernels, axis=0), dm_split) + skip * dm_pair
        ).astype(BF16)
    direct_step = jnp.concatenate(col_sums, axis=0)
    d_cumulative = direct_step * step - row_sums.T[0:8, :]
    d_rate = jnp.dot(d_cumulative, causal.astype(F32), precision=HIGH, preferred_element_type=F32)
    d_raw = (direct_step + growth * d_rate) * (1.0 / (1.0 + jnp.exp(-raw)))
    step_rows[...] = jnp.zeros((128, 128), F32)
    step_rows[own_heads, :] = d_raw
    backs[:, 0:128] = three(dot_rows, d_affinity, c)
    backs[:, 128:256] = three(dot, d_affinity, b)
    backs[:, 256:384] = step_rows[...].T
    lane8 = lax.broadcasted_iota(jnp.int32, (8, 128), 1)
    bias_sum = jnp.sum(d_raw, axis=1, keepdims=True)
    decay_sum = jnp.sum(d_rate * rate, axis=1, keepdims=True)
    small[...] = jnp.zeros((16, 384), F32)
    small[0:1, :] = gain_sum[:, 0:384]
    small[1:2, 0:128] = gain_sum[:, 384:512]
    small[2:3, :] = skip_sum[:, 0:384]
    small[3:4, 0:128] = skip_sum[:, 384:512]
    small[8:16, 0:128] = jnp.where(lane8 == 0, bias_sum, jnp.where(lane8 == 1, decay_sum, 0.0))


def mix_scratch():
    sem = pltpu.SemaphoreType.DMA
    return [
        pltpu.VMEM((128, 512), BF16),
        pltpu.VMEM((128, 512), BF16),
        pltpu.VMEM((128, 512), BF16),
        pltpu.VMEM((128, 384), F32),
        pltpu.VMEM((16, 384), F32),
        pltpu.VMEM((128, 128), F32),
        pltpu.VMEM((128, 512), F32),
        pltpu.VMEM((128, 512), F32),
        pltpu.VMEM((128, 512), F32),
        pltpu.VMEM((8, 128), F32),
        pltpu.VMEM((16, 8, 128), F32),
        sem((16,)), sem((16,)),
    ]


def small_steps(grads, half, total, slots, own, full, c_send, c_recv, s_send, s_recv, g_send, g_recv, e_send, e_recv):
    x_hi, y, core, x_lo, z = coords()
    chip = x_hi * 4 + y
    partner = core_peer()

    def to_chip(j):
        return ((x_hi + j // 4) % 2) * 4 + (y + j % 4) % 4

    def swap():
        return remote(grads.at[1 - core], half, c_send, c_recv, partner)

    def scatter(j):
        return remote(total.at[to_chip(j)], slots.at[chip], s_send.at[j], s_recv.at[j], chip_peer(j))

    def gather(j):
        return remote(own, full.at[core, chip], g_send.at[j], g_recv.at[j], chip_peer(j))

    def share():
        return remote(full.at[core], full.at[core], e_send, e_recv, partner)

    swap().start()
    yield
    swap().wait()
    total[...] = grads[core] + half[...]
    for j in range(1, 8):
        scatter(j).start()
    slots[chip] = total[chip]
    yield
    for j in range(1, 8):
        scatter(j).wait()
    result = slots[0]
    for i in range(1, 8):
        result = result + slots[i]
    own[...] = result
    for j in range(1, 8):
        gather(j).start()
    full[core, chip] = result
    yield
    for j in range(1, 8):
        gather(j).wait()
    share().start()
    yield
    share().wait()


def small_scratch():
    sem = pltpu.SemaphoreType.DMA
    return [
        pltpu.VMEM((2, 8, 40, 384), F32),
        pltpu.VMEM((8, 40, 384), F32),
        pltpu.VMEM((8, 40, 384), F32),
        pltpu.VMEM((8, 40, 384), F32),
        pltpu.VMEM((40, 384), F32),
        pltpu.VMEM((2, 8, 40, 384), F32),
        sem, sem, sem((8,)), sem((8,)), sem((8,)), sem((8,)), sem, sem,
    ]


def output_kernel(
    gate, value, gn, state, heads, gain, slab, s_in, s_out, s_step, tokc_far, upc_far, wcat_far, wof_far,
    layer_out, input_grad, grad_gate, grad_value, grad_output, grad_in, grad_out, grad_step, grad_small,
    all_n, all_g, all_v, part_l, part_d, side, low, grads, grads_in, h_send, h_recv,
    tokc, upc, wcat, wof, loaded, tok_t, up_t, *scratch,
):
    x_hi, y, core, x_lo, z = coords()
    chip = x_hi * 4 + y
    for_mix, scratch = scratch[:13], scratch[13:]
    normed, gate_low, value_low, backs, small = for_mix[:5]
    for_total, scratch = scratch[:8], scratch[8:]
    for_small, scratch = scratch[:14], scratch[14:]
    for_layer, scratch = scratch[:12], scratch[12:]
    for_input, scratch = scratch[:12], scratch[12:]
    gather_layer, gather_input, scratch = scratch[:4], scratch[4:8], scratch[8:]
    for_n, for_g, for_v = scratch[:4], scratch[4:8], scratch[8:]
    partner = core_peer()
    turned, turner, stays = turn_peers()
    devices = [chip_peer(j) for j in range(1, 8)] + [partner] + [tensor_peer(j) for j in range(1, 16)]
    announce(devices)

    @pl.when(jnp.logical_not(stays))
    def _():
        announce([turned, turner])

    loads = [
        pltpu.make_async_copy(source, target, loaded.at[i])
        for i, (source, target) in enumerate(((tokc_far, tokc), (upc_far, upc), (wof_far, wof), (wcat_far, wcat)))
    ]
    for load in loads:
        load.start()
    mixing = mix_steps(gate, value, gn, state, heads, gain, *for_mix)
    drive(mixing)
    gathered(len(devices) + jnp.where(stays, 0, 2))
    drive(mixing)

    def turn_over(array, target):
        def columns(index, carry):
            at = pl.ds(pl.multiple_of(index * 256, 256), 256)
            target[at, :] = array[:, :, at].reshape(1024, 256).T
            return carry

        lax.fori_loop(0, 4, columns, 0)

    loads[0].wait()
    turn_over(tokc, tok_t)
    drive(mixing)
    all_n[chip] = normed[...]

    def chips_of(array):
        return lambda at_side, level: array.at[at_side * 4 + level]

    n_steps = gather_steps(along_y(), chips_of(all_n), *for_n)
    g_steps = gather_steps(along_y(), chips_of(all_g), *for_g)
    v_steps = gather_steps(along_y(), chips_of(all_v), *for_v)
    drive(n_steps)
    finish(mixing)
    all_g[chip] = gate_low[...]
    all_v[chip] = value_low[...]
    drive(n_steps, 2)
    drive(g_steps)
    drive(v_steps)
    back_part, back_full = for_total[0], for_total[7]
    back_part[...] = backs[...].reshape(16, 8, 384)
    back_steps = total_steps(back_part, for_total[1], for_total[2], back_full, *for_total[3:7])
    drive(back_steps)
    loads[1].wait()
    turn_over(upc, up_t)
    finish(n_steps)
    loads[2].wait()

    def store(part, n, block):
        for index in range(8):
            row = 2 * ((y + 4 - index % 4) % 4) + n // 2
            at = pl.ds(pl.multiple_of((n % 2) * 256, 256), 256)
            part[row, index // 4, :, at] = block[128 * index : 128 * index + 128, :]

    def weight_rows(n):
        return pl.ds(pl.multiple_of(n * 256, 256), 256)

    def out_block(n, carry):
        store(part_l, n, dot_cols(all_n[...].reshape(1024, 512), wof[weight_rows(n), :]))
        return carry

    lax.fori_loop(0, 4, out_block, 0)
    theirs = pl.ds(pl.multiple_of((1 - core) * 512, 512), 512)
    mine = pl.ds(pl.multiple_of(core * 512, 512), 512)

    def grad_copy(i):
        return remote(grads.at[i, theirs], grads_in.at[i], h_send.at[i], h_recv.at[i], partner)

    def weight_grad(i, left, right):
        def rows(half):
            def block(index, carry):
                at = pl.ds(pl.multiple_of(half * 512 + index * 256, 256), 256)
                grads[i, at, :] = dot(left[at, :], right[...].reshape(1024, 512))
                return carry

            lax.fori_loop(0, 2, block, 0)

        rows(1 - core)
        grad_copy(i).start()
        rows(core)

    layer_steps = reduce_steps(part_l, *for_layer)
    drive(layer_steps)
    weight_grad(0, up_t, all_n)
    drive(g_steps)
    drive(v_steps)
    drive(layer_steps)
    drive(g_steps)
    drive(v_steps)
    drive(back_steps)
    drive(layer_steps)
    finish(g_steps)
    finish(v_steps)
    loads[3].wait()

    def dense_block(n, carry):
        store(
            part_d, n,
            dot_cols(all_g[...].reshape(1024, 512), wcat[weight_rows(n), 0:512])
            + dot_cols(all_v[...].reshape(1024, 512), wcat[weight_rows(n), 512:1024]),
        )
        return carry

    lax.fori_loop(0, 4, dense_block, 0)
    input_steps = reduce_steps(part_d, *for_input)
    sum_steps = small_steps(*for_small)

    def state_products():
        finish(back_steps)
        low[...] = back_full[...].reshape(128, 384).astype(BF16)
        side[...] = (
            dot_cols(low[:, 0:128], s_in[...]) + dot_cols(low[:, 128:256], s_out[...])
            + dot_cols(low[:, 256:384], s_step[...])
        )
        state_grads = jnp.concatenate(
            [dot_rows(slab[...], low[...]), small[...], jnp.zeros((112, 384), F32)], axis=0
        )
        for_small[0][...] = state_grads.reshape(2, 8, 40, 384)
        drive(sum_steps)

    def blocks_of(result):
        def block(at_side, level, half):
            columns = pl.ds(pl.multiple_of((at_side * 8 + level) * 512, 512), 512)
            return result.at[:, columns] if half is None else result.at[pl.ds(64 * half, 64), columns]

        return block

    own = pl.ds(pl.multiple_of((x_lo * 8 + z) * 512, 512), 512)
    layer_gather = spread_steps(blocks_of(layer_out), *gather_layer)
    input_gather = spread_steps(blocks_of(input_grad), *gather_input)

    def layer_turned():
        finish(layer_steps)
        layer_out[:, own] = for_layer[9][...]

    def input_turned():
        finish(input_steps)
        input_grad[:, own] = (for_input[9][...] + side[...]).astype(BF16)

    def state_results():
        finish(sum_steps)
        summed = for_small[5][...].reshape(640, 384)
        grad_in[...] = summed[0:512, 0:128]
        grad_out[...] = summed[0:512, 128:256]
        grad_step[...] = summed[0:512, 256:384]
        grad_small[...] = summed[512:528, :]

    outs = (grad_output, grad_gate, grad_value)

    def weight_results():
        for i in range(3):
            grad_copy(i).wait_recv()
            outs[i][...] = grads[i, mine, :] + grads_in[i]

    actions = {
        "D": lambda: drive(input_steps),
        "d": input_turned,
        "H": lambda: drive(input_gather),
        "L": lambda: drive(layer_steps),
        "l": layer_turned,
        "G": lambda: drive(layer_gather),
        "g": lambda: finish(layer_gather),
        "B": state_products,
        "S": lambda: drive(sum_steps),
        "s": state_results,
        "1": lambda: weight_grad(1, tok_t, all_g),
        "2": lambda: weight_grad(2, tok_t, all_v),
        "w": weight_results,
    }
    for action in ORDER:
        actions[action]()
    finish(input_gather)
    for i in range(3):
        grad_copy(i).wait_send()


def outputs(*args):
    sem = pltpu.SemaphoreType.DMA
    return pl.pallas_call(
        output_kernel,
        out_shape=(
            jax.ShapeDtypeStruct((128, 8192), BF16),
            jax.ShapeDtypeStruct((128, 8192), BF16),
            jax.ShapeDtypeStruct((512, 512), F32),
            jax.ShapeDtypeStruct((512, 512), F32),
            jax.ShapeDtypeStruct((512, 512), F32),
            jax.ShapeDtypeStruct((512, 128), F32),
            jax.ShapeDtypeStruct((512, 128), F32),
            jax.ShapeDtypeStruct((512, 128), F32),
            jax.ShapeDtypeStruct((16, 384), F32),
        ),
        in_specs=[vmem()] * 10 + [pl.BlockSpec(memory_space=pl.ANY)] * 4,
        out_specs=(vmem(),) * 9,
        scratch_shapes=[
            pltpu.VMEM((8, 128, 512), BF16),
            pltpu.VMEM((8, 128, 512), BF16),
            pltpu.VMEM((8, 128, 512), BF16),
            pltpu.VMEM((8, 2, 128, 512), F32),
            pltpu.VMEM((8, 2, 128, 512), F32),
            pltpu.VMEM((128, 512), F32),
            pltpu.VMEM((128, 384), BF16),
            pltpu.VMEM((3, 1024, 512), F32),
            pltpu.VMEM((3, 512, 512), F32),
            sem((3,)), sem((3,)),
            pltpu.VMEM((8, 128, 1024), BF16),
            pltpu.VMEM((8, 128, 1024), BF16),
            pltpu.VMEM((1024, 1024), BF16),
            pltpu.VMEM((1024, 512), BF16),
            sem((4,)),
            pltpu.VMEM((1024, 1024), BF16),
            pltpu.VMEM((1024, 1024), BF16),
        ]
        + mix_scratch() + total_scratch() + [pltpu.VMEM((16, 8, 384), F32)]
        + small_scratch() + reduce_scratch(BF16) + reduce_scratch(F32) + spread_scratch() * 2
        + gather_scratch(2) * 3,
        compiler_params=params(2),
        cost_estimate=pl.CostEstimate(flops=6 * 10**9, bytes_accessed=300 * 10**6, transcendentals=0),
        name="outputs",
    )(*args)


def settle_kernel(*refs):
    count = (len(refs) - 2) // 3
    ins, outs, boxes = refs[:count], refs[count : 2 * count], refs[2 * count : 3 * count]
    in_sems, out_sems = refs[-2:]
    loads = [pltpu.make_async_copy(ins[i], boxes[i], in_sems.at[i]) for i in range(count)]
    stores = [pltpu.make_async_copy(boxes[i], outs[i], out_sems.at[i]) for i in range(count)]
    for load in loads:
        load.start()
    for load, store in zip(loads, stores):
        load.wait()
        store.start()
    for store in stores:
        store.wait()


def settle(*arrays):
    anywhere = pl.BlockSpec(memory_space=pl.ANY)
    sem = pltpu.SemaphoreType.DMA
    return pl.pallas_call(
        settle_kernel,
        out_shape=tuple(jax.ShapeDtypeStruct(a.shape, a.dtype) for a in arrays),
        in_specs=[anywhere] * len(arrays),
        out_specs=(anywhere,) * len(arrays),
        scratch_shapes=[pltpu.VMEM(a.shape, a.dtype) for a in arrays] + [sem((len(arrays),)), sem((len(arrays),))],
        compiler_params=pltpu.CompilerParams(vmem_limit_bytes=VMEM_LIMIT),
        name="settle",
    )(*arrays)


def per_device(
    tokens_in, proj_gate, proj_value, state_in, state_out, proj_step,
    step_bias, decay_log, skip_scale, norm_gain, proj_output, upstream,
):
    tokc, upc, wcat, wof, slab, gate, value, gn, state = project(
        tokens_in, upstream, proj_gate, proj_value, proj_output, state_in, state_out, proj_step
    )
    heads = jnp.pad(jnp.stack([step_bias, decay_log, skip_scale], axis=1), ((0, 0), (0, 125)))
    *results, sums = outputs(
        gate, value, gn, state, heads, norm_gain.reshape(1, 512), slab, state_in, state_out, proj_step,
        tokc, upc, wcat, wof,
    )
    (
        layer_out, input_grad, grad_gate, grad_value, grad_output, grad_state_in, grad_state_out, grad_step,
    ) = settle(*results)
    grad_gain = jnp.concatenate([sums[0], sums[1, :128]])
    grad_skip = jnp.concatenate([sums[2], sums[3, :128]]).reshape(8, 64).sum(axis=1)
    return (
        layer_out, input_grad, grad_gate, grad_value, grad_output,
        grad_state_in, grad_state_out, grad_step, sums[8:16, 0], sums[8:16, 1], grad_skip, grad_gain,
    )


def solution(mesh):
    block = P("dp", "tensor")
    rows = P("dp", None)
    slab = P("tensor", None)
    vector = P("tensor")
    return jax.shard_map(
        per_device,
        mesh=mesh,
        in_specs=(rows, block, block, slab, slab, slab, vector, vector, vector, vector, block, rows),
        out_specs=(rows, rows, block, block, block, slab, slab, slab, vector, vector, vector, vector),
        check_vma=False,
    )
```
